512 devices in a mesh: facet: 16 (over z_hi, y), sub: 16 (over x, z_lo), vis: 2 (over core).
Axes of the slice: x: 4, y: 4, z: 16 (z_hi: 4, z_lo: 4; z = z_hi * 4 + z_lo), core: 2. Of those that a mesh axis runs over, the one named last changes fastest.
Arguments:
- facet_strips: float32 [16, 512, 4096], P('facet', 'vis'), may hold values from -6 to 6
- taper: float32 [16, 512, 512], P('sub', ('facet', 'vis')), may hold values from 0.3 to 3
- send_pick: int32 [16, 16, 2, 16], P('facet', 'sub', 'vis'), may hold values from 0 to 1
- bl_owner: int32 [16, 16, 2, 8], P('facet', 'sub', 'vis'), may hold values from 0 to 15
- phase_tiles: float32 [16, 16, 2, 8, 64, 128], P('facet', 'sub', 'vis'), may hold values from -6 to 6
- cell_offsets: int32 [16, 16, 2, 8, 2, 1024], P('facet', 'sub', 'vis'), may hold values from 0 to 63
Outputs:
- visibilities: float32 [16, 16, 2, 8, 2, 1024], P('facet', 'sub', 'vis')
The draws below stay inside these ranges and needn't reach their ends.
All inputs are finite; a program needn't handle non-finite values.
Results may differ from the reference program's by a relative error of at most 0.0003.
Values sent between devices are 32-bit elements; how exact they have to be, the bound alone decides.
A program may use at most 64 MiB of HBM per device.

```python
import math
import jax
import jax.numpy as jnp
import numpy as np
from jax import lax

FC = 2048
SG = 512
PS = 64
NVIS = 1024
FH = 512
NBL = 8
PPD = 2
N_FACET = 16
N_SUB = 16
N_VIS = 2


def touch_ends(entries, rng, least, top_value):
    longest = entries.shape.index(max(entries.shape))
    spots = []
    for shift in (0, 1):
        where = [jax.random.randint(jax.random.fold_in(rng, axis), (), 0, length) for axis, length in enumerate(entries.shape)]
        where[longest] = (where[longest] + shift) % entries.shape[longest]
        spots.append(tuple(where))
    return entries.at[spots[0]].set(least).at[spots[1]].set(top_value)


def block_levels(key, shape, cuts, least, largest):
    def one(dim, blocks):
        heights = jax.random.uniform(jax.random.fold_in(jax.random.fold_in(key, 6), dim), (blocks,), jnp.float32, least / len(cuts), largest / len(cuts))
        return jnp.repeat(jnp.exp(heights), shape[dim] // blocks).reshape((-1,) + (1,) * (len(shape) - dim - 1))

    gain = one(*cuts[0])
    for cut in cuts[1:]:
        gain = gain * one(*cut)
    return gain


def cumulative_ranks(number_of, slope):
    portions = [(1 << 20) // math.isqrt(grade ** slope) + 1 for grade in range(1, number_of + 1)]
    width = 1 + sum(portions) // (1 << 30)
    return np.cumsum(np.array([max(1, weight // width) for weight in portions]))


def skewed_ids(key, dims, amount, slope):
    grid = cumulative_ranks(amount, slope)
    pick = jax.random.randint(jax.random.fold_in(key, 1), dims, 0, int(grid[amount - 1]))
    grade = jnp.searchsorted(jnp.asarray(grid, jnp.int32), pick, side="right")
    return jax.random.permutation(jax.random.fold_in(key, 2), amount)[grade].astype(jnp.int32)


def centred(key, dims, scale, most, split=(), kind=jnp.bfloat16):
    result = scale * jax.random.normal(key, dims, jnp.float32)
    if split:
        result = result * block_levels(key, dims, split, -0.22, 0.18)
    return jnp.clip(result, -most, most).astype(kind)


def setup_inputs(seed: int = 0) -> dict:
    key_of = jax.random.split(jax.random.key(seed), 7)
    facet_strips = centred(key_of[0], (N_FACET, FH, 2 * FC), 1.0, 6.0, ((0, 16), (1, 2)), jnp.float32)
    taper = jnp.clip(jnp.exp(math.log(3.0) - 2.3025851 * jax.random.uniform(key_of[1], (N_SUB, SG, SG), jnp.float32) ** block_levels(key_of[1], (N_SUB, SG, SG), ((0, 16), (1, 32)), -0.2, 0.2)), 0.3, 3.0)
    send_pick = touch_ends(jax.random.randint(key_of[2], (N_FACET, N_SUB, N_VIS, N_SUB), 0, PPD), jax.random.fold_in(key_of[2], 1), 0, PPD - 1).astype(jnp.int32)
    bl_owner = touch_ends(skewed_ids(key_of[3], (N_FACET, N_SUB, N_VIS, NBL), N_SUB, 2), jax.random.fold_in(key_of[3], 3), 0, N_SUB - 1).astype(jnp.int32)
    phase_tiles = centred(key_of[4], (N_FACET, N_SUB, N_VIS, NBL, PS, 2 * PS), 1.0, 6.0, ((0, 16), (1, 16), (2, 2)), jnp.float32)
    cell_offsets = touch_ends(jax.random.randint(key_of[5], (N_FACET, N_SUB, N_VIS, NBL, 2, NVIS), 0, PS), jax.random.fold_in(key_of[5], 1), 0, PS - 1).astype(jnp.int32)
    return {"facet_strips": facet_strips, "taper": taper, "send_pick": send_pick, "bl_owner": bl_owner, "phase_tiles": phase_tiles, "cell_offsets": cell_offsets}


sky_cells = 65536
HIGH = lax.Precision.HIGHEST

def sky_turns(left_ids, right_ids):
    left_ids = left_ids % sky_cells
    right_ids = right_ids % sky_cells
    low_byte = right_ids % 256
    high_byte = right_ids // 256
    return (left_ids * low_byte + left_ids * high_byte % 256 * 256) % sky_cells

def sky_table(left_ids, right_ids):
    angles = sky_turns(left_ids, right_ids).astype(jnp.float32) * (2.0 * math.pi / sky_cells)
    return (jnp.cos(angles), -jnp.sin(angles))

def unit_table(left_ids, right_ids, length, orient, factor):
    angles = (left_ids * right_ids % length).astype(jnp.float32) * (2.0 * math.pi / length)
    return (jnp.cos(angles) * factor, jnp.sin(angles) * (orient * factor))

def product(left_op, right_op):
    return jnp.dot(left_op, right_op, precision=HIGH, preferred_element_type=jnp.float32)

def right_mul(values, real_part, imag_part):
    halfway = values.shape[-1] // 2
    val_re = values[:, :halfway]
    val_im = values[:, halfway:]
    return jnp.concatenate([product(val_re, real_part) - product(val_im, imag_part), product(val_re, imag_part) + product(val_im, real_part)], axis=1)

def left_mul(real_part, imag_part, values):
    halfway = values.shape[-1] // 2
    val_re = values[:, :halfway]
    val_im = values[:, halfway:]
    return jnp.concatenate([product(real_part, val_re) - product(imag_part, val_im), product(real_part, val_im) + product(imag_part, val_re)], axis=1)

def strip_tables(facet_index, subgrid, row_start, row_count, col_count, grid_width):
    row_pos = facet_index * 4096 + row_start + jnp.arange(row_count, dtype=jnp.int32)
    col_pos = 5 * facet_index % 16 * 4096 + jnp.arange(col_count, dtype=jnp.int32)
    freqs = jnp.arange(grid_width, dtype=jnp.int32)
    row_freq = subgrid * 4099 + 257 * freqs
    col_freq = subgrid * 1031 + 33 * freqs
    left_re, left_im = sky_table(row_freq[:, None], row_pos[None, :])
    right_re, right_im = sky_table(col_pos[:, None], col_freq[None, :])
    return (left_re, left_im, right_re, right_im)

def degrid(picked, phase_tile, offsets):
    patch_size = picked.shape[-2]
    pick_re = picked[..., :patch_size]
    pick_im = picked[..., patch_size:]
    tile_re = phase_tile[..., :patch_size]
    tile_im = phase_tile[..., patch_size:]
    mixed_re = pick_re * tile_re - pick_im * tile_im
    mixed_im = pick_re * tile_im + pick_im * tile_re
    cells = jnp.arange(patch_size, dtype=jnp.int32)
    u_re, u_im = unit_table(cells[:, None], offsets[..., 0:1, :], patch_size, -1.0, 1.0)
    w_re, w_im = unit_table(cells[:, None], offsets[..., 1:2, :], patch_size, -1.0, 1.0)

    def contract(left_op, right_op):
        return jnp.einsum('...ij,...ik->...jk', left_op, right_op, precision=HIGH, preferred_element_type=jnp.float32)
    along_re = contract(mixed_re, u_re) - contract(mixed_im, u_im)
    along_im = contract(mixed_im, u_re) + contract(mixed_re, u_im)
    vis_re = lax.optimization_barrier(jnp.sum(along_re * w_re - along_im * w_im, axis=-2)) / patch_size
    vis_im = lax.optimization_barrier(jnp.sum(along_re * w_im + along_im * w_re, axis=-2)) / patch_size
    return jnp.stack([vis_re, vis_im], axis=-2)

def reference(facet_strips, taper, send_pick, bl_owner, phase_tiles, cell_offsets):
    scaling = 1.0 / math.sqrt(FH * FC * N_FACET)
    cell_index = jnp.arange(SG, dtype=jnp.int32)
    q_re, q_im = unit_table(cell_index[:, None], cell_index[None, :], SG, 1.0, 1.0 / math.sqrt(SG))
    facet_ids = jnp.arange(N_FACET, dtype=jnp.int32)

    def one_grid(inputs):
        subgrid, window = inputs

        def add_facet(running, element):
            strip_data, facet_index = element
            left_re, left_im, right_re, right_im = strip_tables(facet_index, subgrid, 0, FH, FC, SG)
            strip_term = left_mul(left_re, left_im, right_mul(strip_data, right_re, right_im)) * scaling
            return (running + strip_term, None)
        summed, _ = lax.scan(add_facet, jnp.zeros((SG, 2 * SG), jnp.float32), (facet_strips, facet_ids))
        tapered = summed * jnp.concatenate([window, window], axis=1)
        return left_mul(q_re, q_im, right_mul(tapered, q_re, q_im))
    grids = lax.map(one_grid, (jnp.arange(N_SUB, dtype=jnp.int32), taper))
    per_side = SG // PS
    grid_re = grids[:, :, :SG].reshape(N_SUB, per_side, PS, per_side, PS).transpose(0, 1, 3, 2, 4)
    grid_im = grids[:, :, SG:].reshape(N_SUB, per_side, PS, per_side, PS).transpose(0, 1, 3, 2, 4)
    patches = jnp.concatenate([grid_re, grid_im], axis=-1).reshape(N_SUB, per_side * per_side, PS, 2 * PS)
    facet_col = jnp.arange(N_FACET, dtype=jnp.int32)[:, None, None, None]
    sub_col = jnp.arange(N_SUB, dtype=jnp.int32)[None, :, None, None]
    core_col = jnp.arange(N_VIS, dtype=jnp.int32)[None, None, :, None]
    chosen = send_pick[facet_col, bl_owner, core_col, sub_col]
    slots = ((facet_col * N_VIS + core_col) * PPD + chosen).astype(jnp.int32)
    slots = jnp.broadcast_to(slots, bl_owner.shape)

    def one_facet(inputs):
        owners, slot_row, tile_row, offset_row = inputs
        return degrid(patches[owners, slot_row], tile_row, offset_row)
    return lax.map(one_facet, (bl_owner, slots, phase_tiles, cell_offsets))
```

```python
import functools
import math

import jax
import jax.numpy as jnp
import ml_dtypes
import numpy as np
from jax import lax
from jax.experimental import pallas as pl
from jax.experimental.pallas import tpu as pltpu
from jax.sharding import PartitionSpec as P

MESH = pl.DeviceIdType.MESH
F32 = jnp.float32
BF16 = jnp.bfloat16
VM = pl.BlockSpec(memory_space=pltpu.VMEM)
SCALE = 1.0 / math.sqrt(512 * 2048 * 16)


def halves(table):
    high = table.astype(np.float32).astype(ml_dtypes.bfloat16)
    low = (table - high.astype(np.float64)).astype(ml_dtypes.bfloat16)
    return high, low


@functools.lru_cache(None)
def column_table():
    freq = np.arange(512)[:, None]
    cols = np.arange(2048)[None, :]
    angle = (33 * freq * cols % 65536) * (2.0 * np.pi / 65536)
    both = np.stack([np.cos(angle).reshape(32, 16, 2048), -np.sin(angle).reshape(32, 16, 2048)], 1)
    return halves(both.reshape(1024, 2048))


@functools.lru_cache(None)
def row_table():
    rows = np.arange(256)[:, None]
    freq = np.arange(512)[None, :]
    angle = (257 * freq * rows % 65536) * (2.0 * np.pi / 65536)
    return halves(np.concatenate([np.cos(angle), -np.sin(angle)], 1))


@functools.lru_cache(None)
def grid_table():
    left = np.arange(512)[:, None]
    right = np.arange(512)[None, :]
    angle = (left * right % 512) * (2.0 * np.pi / 512)
    scale = 1.0 / math.sqrt(512)
    both = np.stack(
        [np.cos(angle).reshape(512, 8, 64) * scale, np.sin(angle).reshape(512, 8, 64) * scale], 2
    )
    return halves(both.reshape(512, 1024))


@functools.lru_cache(None)
def cell_tables():
    left = np.arange(64)[:, None]
    right = np.arange(64)[None, :]
    angle = (left * right % 64) * (2.0 * np.pi / 64)
    cos, sin = np.cos(angle) / 8.0, -np.sin(angle) / 8.0
    square = np.concatenate(
        [np.concatenate([cos, sin], 1), np.concatenate([-sin, cos], 1)], 0
    )
    flat = np.concatenate([cos, sin], 1)
    return halves(square) + halves(flat)


def split(value):
    high = value.astype(BF16)
    return high, (value - high.astype(F32)).astype(BF16)


def dot(left, right):
    return jnp.dot(left, right, preferred_element_type=F32)


def dot_t(left, right):
    return lax.dot_general(left, right, (((1,), (1,)), ((), ())), preferred_element_type=F32)


def dot3(left, right_high, right_low):
    high, low = split(left)
    return dot(high, right_high) + dot(low, right_high) + dot(high, right_low)


def turned(turns, modulus):
    angles = (turns & (modulus - 1)).astype(F32) * (2.0 * math.pi / modulus)
    return jnp.cos(angles), -jnp.sin(angles)


def iota(shape, dim):
    return lax.broadcasted_iota(jnp.int32, shape, dim)


def strip_kernel(place, re_ref, im_ref, th_ref, tl_ref, lh_ref, ll_ref, out_ref, acc):
    step = pl.program_id(0)
    facet, sub, core = place[0], place[1], place[2]
    width = re_ref.shape[1]
    cols = step * width + iota((8, width), 1)
    c_re, c_im = turned(sub * 1031 * cols, 65536)
    c_re, c_im = c_re[0:1], c_im[0:1]
    s_re, s_im = re_ref[...], im_ref[...]
    moved = jnp.concatenate([s_re * c_re - s_im * c_im, s_re * c_im + s_im * c_re], 0)
    high, low = split(moved)
    t_high = th_ref[...]
    more = dot_t(t_high, high) + dot_t(t_high, low) + dot_t(tl_ref[...], high)

    @pl.when(step == 0)
    def _():
        acc[...] = more

    @pl.when(step > 0)
    def _():
        acc[...] += more

    @pl.when(step == pl.num_programs(0) - 1)
    def _():
        rows = core * 256 + iota((8, 256), 1)
        r_re, r_im = turned(sub * 4099 * rows, 65536)
        r_re, r_im = r_re[0:1], r_im[0:1]
        freq = iota((16, 512), 1)
        other = iota((16, 512), 0)
        turn = facet * ((freq + 5 * other + 6 * sub) & 15) * 16 + freq * core
        w_re, w_im = turned(turn, 256)
        w_re, w_im = w_re * SCALE, w_im * SCALE

        def chunk(index, carry):
            where = pl.ds(pl.multiple_of(index * 256, 256), 256)
            part = acc[where, :].reshape(8, 2, 16, 512)
            q_re, q_im = part[:, 0], part[:, 1]
            a_re = q_re[..., :256] - q_im[..., 256:]
            a_im = q_re[..., 256:] + q_im[..., :256]
            turned_re = a_re * r_re - a_im * r_im
            turned_im = a_re * r_im + a_im * r_re
            both = jnp.stack([turned_re, turned_im], 1).reshape(256, 256)
            prod = dot3(both, lh_ref[...], ll_ref[...]).reshape(8, 2, 16, 1024)
            p_re, p_im = prod[:, 0], prod[:, 1]
            o_re = p_re[..., :512] - p_im[..., 512:]
            o_im = p_re[..., 512:] + p_im[..., :512]
            out_re = o_re * w_re - o_im * w_im
            out_im = o_re * w_im + o_im * w_re
            out_ref[where, :] = jnp.stack([out_re, out_im], 1).reshape(256, 512)
            return carry

        lax.fori_loop(0, 4, chunk, 0)


def strip_part(place, strip):
    steps = 4
    width = 2048 // steps
    t_high, t_low = (jnp.asarray(x) for x in column_table())
    l_high, l_low = (jnp.asarray(x) for x in row_table())
    whole = pl.BlockSpec((256, 1024), lambda i, p: (0, 0))
    return pl.pallas_call(
        strip_kernel,
        out_shape=jax.ShapeDtypeStruct((1024, 512), F32),
        grid_spec=pltpu.PrefetchScalarGridSpec(
            num_scalar_prefetch=1,
            grid=(steps,),
            in_specs=[
                pl.BlockSpec((256, width), lambda i, p: (0, i)),
                pl.BlockSpec((256, width), lambda i, p: (0, i + steps)),
                pl.BlockSpec((1024, width), lambda i, p: (0, i)),
                pl.BlockSpec((1024, width), lambda i, p: (0, i)),
                whole,
                whole,
            ],
            out_specs=pl.BlockSpec((1024, 512), lambda i, p: (0, 0)),
            scratch_shapes=[pltpu.VMEM((1024, 512), F32)],
        ),
        compiler_params=pltpu.CompilerParams(vmem_limit_bytes=56 << 20),
    )(place, strip, strip, t_high, t_low, l_high, l_low)


def here():
    facet, sub, core = lax.axis_index("facet"), lax.axis_index("sub"), lax.axis_index("vis")
    return facet // 4, facet % 4, sub // 4, sub % 4, core


def sum_kernel(
    part, tap, sum_out, tap_out, got_core, half, got_y, to_z, got_z,
    core_send, core_recv, y_send, y_recv, z_send, z_recv, t_send, t_recv,
):
    z, y, _, _, c = here()
    me = (z * 4 + y) * 2 + c
    barrier = pltpu.get_barrier_semaphore()

    def greet(step, carry):
        peer = (me + step) % 32
        pl.semaphore_signal(
            barrier, inc=1, device_id={"facet": peer // 2, "vis": peer % 2}, device_id_type=MESH
        )
        return carry

    lax.fori_loop(1, 32, greet, 0)
    pl.semaphore_wait(barrier, 31)

    def core_copy(at):
        return pltpu.make_async_remote_copy(
            src_ref=part.at[1 - c, :, at], dst_ref=got_core.at[:, at],
            send_sem=core_send.at[at], recv_sem=core_recv.at[at],
            device_id={"vis": 1 - c}, device_id_type=MESH,
        )

    def y_copy(dy, at):
        to = (y + dy) % 4
        return pltpu.make_async_remote_copy(
            src_ref=half.at[to, at], dst_ref=got_y.at[dy - 1, at],
            send_sem=y_send.at[dy - 1, at], recv_sem=y_recv.at[dy - 1, at],
            device_id={"facet": z * 4 + to}, device_id_type=MESH,
        )

    def z_copy(dz):
        to = (z + dz) % 4
        return pltpu.make_async_remote_copy(
            src_ref=to_z.at[dz - 1], dst_ref=got_z.at[dz - 1],
            send_sem=z_send.at[dz - 1], recv_sem=z_recv.at[dz - 1],
            device_id={"facet": to * 4 + y}, device_id_type=MESH,
        )

    def tap_copy(step):
        peer = (me + step) % 32
        block = (peer % 2) * 16 + (peer // 2 % 4) * 4 + peer // 8
        return pltpu.make_async_remote_copy(
            src_ref=tap.at[block], dst_ref=tap_out.at[me],
            send_sem=t_send.at[step], recv_sem=t_recv.at[step],
            device_id={"facet": peer // 2, "vis": peer % 2}, device_id_type=MESH,
        )

    def tap_arrival(step):
        source = (me - step + 32) % 32
        return pltpu.make_async_remote_copy(
            src_ref=tap.at[0], dst_ref=tap_out.at[source],
            send_sem=t_send.at[step], recv_sem=t_recv.at[step],
            device_id={"facet": source // 2, "vis": source % 2}, device_id_type=MESH,
        )

    order = (2, 1, 3, 0)
    for dz in order:
        core_copy((z + dz) % 4).start()

    def tap_start(step, carry):
        tap_copy(step).start()
        return carry

    lax.fori_loop(1, 32, tap_start, 0)
    tap_out[me] = tap[c * 16 + y * 4 + z]
    for dz in order:
        at = (z + dz) % 4
        core_copy(at).wait()
        for dy in (2, 1, 3, 0):
            to = (y + dy) % 4
            half[to, at] = part[c, to, at] + got_core[to, at]
            if dy:
                y_copy(dy, at).start()
    for dz in order:
        at = (z + dz) % 4
        for dy in (1, 3, 2):
            y_copy(dy, at).wait()
        total = (half[y, at] + got_y[0, at]) + (got_y[1, at] + got_y[2, at])
        if dz:
            to_z[dz - 1] = total
            z_copy(dz).start()
        else:
            sum_out[...] = total

    def tap_wait(step, carry):
        tap_copy(step).wait_send()
        tap_arrival(step).wait_recv()
        return carry

    lax.fori_loop(1, 32, tap_wait, 0)
    for dz in (1, 3, 2):
        z_copy(dz).wait()
    sum_out[...] += got_z[0] + got_z[1] + got_z[2]


def sum_over_facets(part, tap):
    dma = pltpu.SemaphoreType.DMA
    return pl.pallas_call(
        sum_kernel,
        out_shape=(
            jax.ShapeDtypeStruct((32, 512), F32),
            jax.ShapeDtypeStruct((32, 2, 128), F32),
        ),
        in_specs=[VM, VM],
        out_specs=(VM, VM),
        scratch_shapes=[
            pltpu.VMEM((4, 4, 32, 512), F32),
            pltpu.VMEM((4, 4, 32, 512), F32),
            pltpu.VMEM((3, 4, 32, 512), F32),
            pltpu.VMEM((3, 32, 512), F32),
            pltpu.VMEM((3, 32, 512), F32),
            dma((4,)), dma((4,)), dma((3, 4)), dma((3, 4)), dma((3,)), dma((3,)),
            dma((32,)), dma((32,)),
        ],
        compiler_params=pltpu.CompilerParams(
            collective_id=0, has_side_effects=True, vmem_limit_bytes=40 << 20
        ),
    )(part, tap)


def swapped(top, bottom):
    sign = jnp.where(iota(top.shape, 1) < 64, -1.0, 1.0).astype(F32)
    return top + pltpu.roll(bottom, 64, 1) * sign


def grid_kernel(
    sums, window, ph, pw, out, ubuf, zbuf, ybuf, z_send, z_recv, y_send, y_recv
):
    z, y, _, _, c = here()
    barrier = pltpu.get_barrier_semaphore()
    for dz in (1, 2, 3):
        pl.semaphore_signal(
            barrier, inc=1, device_id={"facet": (z + dz) % 4 * 4 + y}, device_id_type=MESH
        )
    near = [(dy, dc) for dy in range(4) for dc in range(2) if dy or dc]
    for dy, dc in near:
        pl.semaphore_signal(
            barrier, inc=1,
            device_id={"facet": z * 4 + (y + dy) % 4, "vis": (c + dc) % 2}, device_id_type=MESH,
        )
    taper = window[...]
    tapered = sums[...] * jnp.concatenate([taper, taper], 0)
    prod = dot3(tapered, ph[...], pw[...])
    for block in range(8):
        where = slice(block * 128, block * 128 + 128)
        ubuf[block // 2, block % 2] = swapped(prod[:16, where], prod[16:, where])
    pl.semaphore_wait(barrier, 10)

    def z_copy(dz):
        to = (z + dz) % 4
        return pltpu.make_async_remote_copy(
            src_ref=ubuf.at[to], dst_ref=zbuf.at[z],
            send_sem=z_send.at[dz - 1], recv_sem=z_recv.at[dz - 1],
            device_id={"facet": to * 4 + y}, device_id_type=MESH,
        )

    def z_arrival(dz):
        source = (z - dz + 4) % 4
        return pltpu.make_async_remote_copy(
            src_ref=ubuf.at[source], dst_ref=zbuf.at[source],
            send_sem=z_send.at[dz - 1], recv_sem=z_recv.at[dz - 1],
            device_id={"facet": source * 4 + y}, device_id_type=MESH,
        )

    def y_copy(index):
        dy, dc = near[index]
        to = (y + dy) % 4
        return pltpu.make_async_remote_copy(
            src_ref=zbuf.at[:, to // 2], dst_ref=ybuf.at[c, y],
            send_sem=y_send.at[index], recv_sem=y_recv.at[index],
            device_id={"facet": z * 4 + to, "vis": (c + dc) % 2}, device_id_type=MESH,
        )

    def y_arrival(index):
        dy, dc = near[index]
        source = (y - dy + 4) % 4
        return pltpu.make_async_remote_copy(
            src_ref=zbuf.at[:, 0], dst_ref=ybuf.at[(c + dc) % 2, source],
            send_sem=y_send.at[index], recv_sem=y_recv.at[index],
            device_id={"facet": z * 4 + source, "vis": (c + dc) % 2}, device_id_type=MESH,
        )

    for dz in (2, 1, 3):
        z_copy(dz).start()
    zbuf[z] = ubuf[z]
    for dz in (1, 3, 2):
        z_arrival(dz).wait_recv()
    for index in range(7):
        y_copy(index).start()
    ybuf[c, y] = zbuf[:, y // 2]
    for dz in (1, 2, 3):
        z_copy(dz).wait_send()
    for index in range(7):
        y_copy(index).wait_send()
        y_arrival(index).wait_recv()
    cols = ybuf[...].reshape(512, 128).T
    where = pl.ds(pl.multiple_of(((y % 2) * 2 + c) * 256, 256), 256)
    prod = dot3(cols, ph[:, where], pw[:, where])
    for j in range(2):
        where = slice(j * 128, j * 128 + 128)
        out[j] = swapped(prod[:64, where], prod[64:, where])


def grid_patches(sums, window):
    dma = pltpu.SemaphoreType.DMA
    ph, pw = (jnp.asarray(x) for x in grid_table())
    return pl.pallas_call(
        grid_kernel,
        out_shape=jax.ShapeDtypeStruct((2, 64, 128), F32),
        in_specs=[VM] * 4,
        out_specs=VM,
        scratch_shapes=[
            pltpu.VMEM((4, 2, 16, 128), F32),
            pltpu.VMEM((4, 2, 16, 128), F32),
            pltpu.VMEM((2, 4, 4, 16, 128), F32),
            dma((3,)), dma((3,)), dma((7,)), dma((7,)),
        ],
        compiler_params=pltpu.CompilerParams(
            collective_id=1, has_side_effects=True, vmem_limit_bytes=40 << 20
        ),
    )(sums, window, ph, pw)


def patch_kernel(
    own, picks, out, zpatch, zpick, staged, z_send, z_recv, p_send, p_recv, x_send, x_recv
):
    _, _, x, z, _ = here()
    barrier = pltpu.get_barrier_semaphore()
    for step in (1, 2, 3):
        pl.semaphore_signal(
            barrier, inc=1, device_id={"sub": x * 4 + (z + step) % 4}, device_id_type=MESH
        )
        pl.semaphore_signal(
            barrier, inc=1, device_id={"sub": (x + step) % 4 * 4 + z}, device_id_type=MESH
        )
    pl.semaphore_wait(barrier, 6)

    def z_copies(dz):
        to = (z + dz) % 4
        device = {"sub": x * 4 + to}
        return (
            pltpu.make_async_remote_copy(
                src_ref=own, dst_ref=zpatch.at[dz - 1], send_sem=z_send.at[dz - 1],
                recv_sem=z_recv.at[dz - 1], device_id=device, device_id_type=MESH,
            ),
            pltpu.make_async_remote_copy(
                src_ref=picks.at[to], dst_ref=zpick.at[dz - 1], send_sem=p_send.at[dz - 1],
                recv_sem=p_recv.at[dz - 1], device_id=device, device_id_type=MESH,
            ),
        )

    def x_copy(dx, dz):
        source = (z - dz + 4) % 4
        return pltpu.make_async_remote_copy(
            src_ref=staged.at[dx - 1, dz], dst_ref=out.at[x * 4 + source],
            send_sem=x_send.at[dx - 1, dz], recv_sem=x_recv.at[dx - 1, dz],
            device_id={"sub": (x + dx) % 4 * 4 + z}, device_id_type=MESH,
        )

    def x_arrival(dx, dz):
        origin = (x - dx + 4) % 4
        source = (z - dz + 4) % 4
        return pltpu.make_async_remote_copy(
            src_ref=staged.at[dx - 1, dz], dst_ref=out.at[origin * 4 + source],
            send_sem=x_send.at[dx - 1, dz], recv_sem=x_recv.at[dx - 1, dz],
            device_id={"sub": origin * 4 + z}, device_id_type=MESH,
        )

    for dz in (2, 1, 3):
        for copy in z_copies(dz):
            copy.start()
    for dz in (0, 1, 3, 2):
        source = (z - dz + 4) % 4
        if dz:
            for copy in z_copies(dz):
                copy.wait_recv()
            first, second, table = zpatch[dz - 1, 0], zpatch[dz - 1, 1], zpick.at[dz - 1]
        else:
            first, second, table = own[0], own[1], picks.at[z]
        for dx in (2, 1, 3, 0):
            chosen = table[pl.ds((x + dx) % 4, 1), :]
            value = jnp.where(jnp.broadcast_to(chosen, first.shape) > 0.5, second, first)
            if dx:
                staged[dx - 1, dz] = value
                x_copy(dx, dz).start()
            else:
                out[x * 4 + source] = value
    for dz in (1, 2, 3):
        for copy in z_copies(dz):
            copy.wait_send()
    for dz in (0, 1, 3, 2):
        for dx in (1, 3, 2):
            x_copy(dx, dz).wait_send()
            x_arrival(dx, dz).wait_recv()


def share_patches(own, picks):
    dma = pltpu.SemaphoreType.DMA
    return pl.pallas_call(
        patch_kernel,
        out_shape=jax.ShapeDtypeStruct((16, 64, 128), F32),
        in_specs=[VM, VM],
        out_specs=VM,
        scratch_shapes=[
            pltpu.VMEM((3, 2, 64, 128), F32),
            pltpu.VMEM((3, 8, 128), F32),
            pltpu.VMEM((3, 4, 64, 128), F32),
            dma((3,)), dma((3,)), dma((3,)), dma((3,)), dma((3, 4)), dma((3, 4)),
        ],
        compiler_params=pltpu.CompilerParams(
            collective_id=2, has_side_effects=True, vmem_limit_bytes=40 << 20
        ),
    )(own, picks)


def degrid_kernel(owners, patches, tiles, offsets, eh, el, fh, fl, out):
    low_lane = iota((64, 128), 1) < 64
    cells = iota((64, 1024), 0)

    def one(base, carry):
        patch = patches[owners[base]]
        tile = tiles[base]
        straight = patch * tile
        crossed = patch * pltpu.roll(tile, 64, 1)
        mixed = jnp.where(
            low_lane, straight - pltpu.roll(straight, 64, 1), crossed + pltpu.roll(crossed, 64, 1)
        )
        along = dot3(mixed, eh[...], el[...])
        quad = dot3(along.T, fh[...], fl[...])
        re = quad[:64, :64] - quad[64:, 64:]
        im = quad[:64, 64:] + quad[64:, :64]
        high, low = split(jnp.concatenate([re, im], 0))
        pair = jnp.concatenate([high, low], 1)
        spot = offsets[base]
        hot = jnp.where(cells == spot[0:1], 1.0, 0.0).astype(BF16)
        rows = dot(pair, jnp.concatenate([hot, hot], 0))
        hit = cells == spot[1:2]
        vis_re = jnp.sum(jnp.where(hit, rows[:64], 0.0), 0, keepdims=True)
        vis_im = jnp.sum(jnp.where(hit, rows[64:], 0.0), 0, keepdims=True)
        out[base] = jnp.concatenate([vis_re, vis_im], 0)
        return carry

    lax.fori_loop(0, 8, one, 0)


def degrid(owners, patches, tiles, offsets):
    tables = [jnp.asarray(x) for x in cell_tables()]
    return pl.pallas_call(
        degrid_kernel,
        out_shape=jax.ShapeDtypeStruct((8, 2, 1024), F32),
        in_specs=[pl.BlockSpec(memory_space=pltpu.SMEM)] + [VM] * 7,
        out_specs=VM,
        compiler_params=pltpu.CompilerParams(vmem_limit_bytes=40 << 20),
    )(owners, patches, tiles, offsets, *tables)


def local(facet_strips, taper, send_pick, bl_owner, phase_tiles, cell_offsets):
    place = jnp.stack(
        [lax.axis_index("facet"), lax.axis_index("sub"), lax.axis_index("vis")]
    ).astype(jnp.int32)
    part = strip_part(place, facet_strips[0])
    tap = taper[0].T.reshape(32, 2, 128)
    sums, windows = sum_over_facets(part.reshape(2, 4, 4, 32, 512), tap)
    window = windows.reshape(32, 16, 16).transpose(1, 0, 2).reshape(16, 512)
    own = grid_patches(sums, window)
    picks = send_pick[0, 0, 0].astype(F32).reshape(4, 4).T
    picks = jnp.broadcast_to(jnp.pad(picks, ((0, 0), (0, 4)))[:, :, None], (4, 8, 128))
    patches = share_patches(own, picks)
    result = degrid(bl_owner[0, 0, 0], patches, phase_tiles[0, 0, 0], cell_offsets[0, 0, 0])
    return result[None, None, None]


def solution(mesh):
    placed = (
        P("facet", "vis", None),
        P("sub", ("facet", "vis"), None),
        P("facet", "sub", "vis", None),
        P("facet", "sub", "vis", None),
        P("facet", "sub", "vis", None, None, None),
        P("facet", "sub", "vis", None, None, None),
    )
    return jax.shard_map(
        local,
        mesh=mesh,
        in_specs=placed,
        out_specs=P("facet", "sub", "vis", None, None, None),
        check_vma=False,
    )
```

```python
import functools
import math

import jax
import jax.numpy as jnp
import ml_dtypes
import numpy as np
from jax import lax
from jax.experimental import pallas as pl
from jax.experimental.pallas import tpu as pltpu
from jax.sharding import PartitionSpec as P

MESH = pl.DeviceIdType.MESH
F32 = jnp.float32
BF16 = jnp.bfloat16
VM = pl.BlockSpec(memory_space=pltpu.VMEM)
SCALE = 1.0 / math.sqrt(512 * 2048 * 16)


def halves(table):
    high = table.astype(np.float32).astype(ml_dtypes.bfloat16)
    low = (table - high.astype(np.float64)).astype(ml_dtypes.bfloat16)
    return high, low


@functools.lru_cache(None)
def column_table():
    freq = np.arange(512).reshape(2, 4, 4, 16).transpose(2, 0, 1, 3).reshape(4, 1, 128)
    cols = np.arange(2048)[None, :, None]
    angle = (33 * freq * cols % 65536) * (2.0 * np.pi / 65536)
    return halves(np.concatenate([np.cos(angle), -np.sin(angle)], 2))


@functools.lru_cache(None)
def row_table():
    rows = np.arange(256)[:, None]
    freq = np.arange(512)[None, :]
    angle = (257 * freq * rows % 65536) * (2.0 * np.pi / 65536)
    return halves(np.concatenate([np.cos(angle), -np.sin(angle)], 1))


@functools.lru_cache(None)
def grid_table():
    left = np.arange(512)[:, None]
    right = np.arange(512)[None, :]
    angle = (left * right % 512) * (2.0 * np.pi / 512)
    scale = 1.0 / math.sqrt(512)
    both = np.stack(
        [np.cos(angle).reshape(512, 8, 64) * scale, np.sin(angle).reshape(512, 8, 64) * scale], 2
    )
    return halves(both.reshape(512, 1024))


@functools.lru_cache(None)
def cell_tables():
    left = np.arange(64)[:, None]
    right = np.arange(64)[None, :]
    angle = (left * right % 64) * (2.0 * np.pi / 64)
    cos, sin = np.cos(angle) / 8.0, -np.sin(angle) / 8.0
    square = np.concatenate(
        [np.concatenate([cos, sin], 1), np.concatenate([-sin, cos], 1)], 0
    )
    flat = np.concatenate([cos, sin], 1)
    return halves(square) + halves(flat)


def split(value):
    high = value.astype(BF16)
    return high, (value - high.astype(F32)).astype(BF16)


def dot(left, right):
    return jnp.dot(left, right, preferred_element_type=F32)


def dot_t(left, right):
    return lax.dot_general(left, right, (((1,), (1,)), ((), ())), preferred_element_type=F32)


def dot3(left, right_high, right_low):
    high, low = split(left)
    return dot(high, right_high) + dot(low, right_high) + dot(high, right_low)


def turned(turns, modulus):
    angles = (turns & (modulus - 1)).astype(F32) * (2.0 * math.pi / modulus)
    return jnp.cos(angles), -jnp.sin(angles)


def iota(shape, dim):
    return lax.broadcasted_iota(jnp.int32, shape, dim)


def here():
    facet, sub, core = lax.axis_index("facet"), lax.axis_index("sub"), lax.axis_index("vis")
    return facet // 4, facet % 4, sub // 4, sub % 4, core


def swapped(top, bottom):
    sign = jnp.where(iota(top.shape, 1) < 64, -1.0, 1.0).astype(F32)
    return top + pltpu.roll(bottom, 64, 1) * sign


PIECES = 4
near = [(dy, dc) for dy in range(4) for dc in range(2) if dy or dc]


def remote(src, dst, send, recv, device):
    return pltpu.make_async_remote_copy(
        src_ref=src, dst_ref=dst, send_sem=send, recv_sem=recv,
        device_id=device, device_id_type=MESH,
    )


def placed_taper(blocks):
    values = jnp.concatenate([blocks[:, 0, :], blocks[:, 1, :]], 1).T
    high = values.astype(BF16)
    middle, low = split(values - high.astype(F32))
    spread = jnp.where(iota((32, 512), 1) // 16 == iota((32, 512), 0), 1.0, 0.0).astype(BF16)
    wide = dot(high, spread) + (dot(middle, spread) + dot(low, spread))
    hit = (iota((256, 512), 0) & 15) == (iota((256, 512), 1) & 15)
    return jnp.sum(jnp.where(hit, wide, 0.0).reshape(16, 16, 512), 1)


def patch_kernel(
    strip, th_hbm, tl_hbm, lh_ref, ll_ref, tap, ph, pw, pick_ref, out,
    raw, xh, xl, th, tl, part, got_core, got_y, tot, got_z, tap_out,
    ubuf, zbuf, ybuf, own, picks, zpatch, zpick, staged,
    raw_sem, t_sem, core_send, core_recv, y_send, y_recv, z_send, z_recv, tap_send, tap_recv,
    uz_send, uz_recv, uy_send, uy_recv, w_send, w_recv, p_send, p_recv, x_send, x_recv,
):
    z, y, x, w, c = here()
    facet, sub, core = lax.axis_index("facet"), lax.axis_index("sub"), c
    me = (z * 4 + y) * 2 + c
    width = 2048 // PIECES
    order = (2, 1, 3, 0)

    def raw_copy(index):
        where = pl.ds(index * width, width)
        return pltpu.make_async_copy(strip.at[:, where], raw.at[:, where], raw_sem.at[index])

    def t_copies(dz):
        at = (z + dz) % 4
        return (
            pltpu.make_async_copy(th_hbm.at[at], th.at[dz], t_sem.at[dz, 0]),
            pltpu.make_async_copy(tl_hbm.at[at], tl.at[dz], t_sem.at[dz, 1]),
        )

    for index in range(PIECES):
        raw_copy(index).start()
        raw_copy(index + PIECES).start()
        if index == 0:
            for copy in t_copies(order[0]):
                copy.start()
    for dz in order[1:]:
        for copy in t_copies(dz):
            copy.start()

    barrier = pltpu.get_barrier_semaphore()

    def greet(step, carry):
        peer = (me + step) % 32
        pl.semaphore_signal(
            barrier, inc=1, device_id={"facet": peer // 2, "vis": peer % 2}, device_id_type=MESH
        )
        return carry

    lax.fori_loop(1, 32, greet, 0)
    for step in (1, 2, 3):
        pl.semaphore_signal(
            barrier, inc=1, device_id={"sub": x * 4 + (w + step) % 4}, device_id_type=MESH
        )
        pl.semaphore_signal(
            barrier, inc=1, device_id={"sub": (x + step) % 4 * 4 + w}, device_id_type=MESH
        )

    def core_copy(dz):
        return remote(
            part.at[dz, 1 - c], got_core.at[dz], core_send.at[dz], core_recv.at[dz], {"vis": 1 - c}
        )

    def y_copy(dz, dy):
        to = (y + dy) % 4
        return remote(
            part.at[dz, c, to], got_y.at[dz, dy - 1], y_send.at[dz, dy - 1],
            y_recv.at[dz, dy - 1], {"facet": z * 4 + to},
        )

    def z_copy(dz):
        return remote(
            tot.at[dz], got_z.at[dz - 1], z_send.at[dz - 1], z_recv.at[dz - 1],
            {"facet": (z + dz) % 4 * 4 + y},
        )

    def tap_copy(step):
        peer = (me + step) % 32
        block = (peer % 2) * 16 + (peer // 2 % 4) * 4 + peer // 8
        return remote(
            tap.at[block], tap_out.at[me], tap_send.at[step], tap_recv.at[step],
            {"facet": peer // 2, "vis": peer % 2},
        )

    def tap_arrival(step):
        source = (me - step + 32) % 32
        return remote(
            tap.at[0], tap_out.at[source], tap_send.at[step], tap_recv.at[step],
            {"facet": source // 2, "vis": source % 2},
        )

    def after_core(dz):
        core_copy(dz).wait()
        part[dz, c] = part[dz, c] + got_core[dz]
        for dy in (2, 1, 3):
            y_copy(dz, dy).start()

    def after_y(dz):
        for dy in (1, 3, 2):
            y_copy(dz, dy).wait()
        tot[dz] = (part[dz, c, y] + got_y[dz, 0]) + (got_y[dz, 1] + got_y[dz, 2])
        if dz:
            z_copy(dz).start()

    rows = core * 256 + iota((8, 256), 1)
    r_re, r_im = turned(sub * 4099 * rows, 65536)
    r_re, r_im = r_re[0:1], r_im[0:1]
    freq = iota((16, 512), 1)
    other = iota((16, 512), 0)
    turn = facet * ((freq + 5 * other + 6 * sub) & 15) * 16 + freq * core
    w_re, w_im = turned(turn, 256)
    w_re, w_im = (w_re * SCALE)[None], (w_im * SCALE)[None]

    def finish(dz, acc):
        top, bottom = acc[:256], acc[256:]
        a_re = (top[:, :128] - bottom[:, 128:]).T
        a_im = (top[:, 128:] + bottom[:, :128]).T
        both = jnp.concatenate([a_re * r_re - a_im * r_im, a_re * r_im + a_im * r_re], 0)
        prod = dot3(both, lh_ref[...], ll_ref[...])
        p_re, p_im = prod[:128], prod[128:]
        o_re = (p_re[:, :512] - p_im[:, 512:]).reshape(8, 16, 512)
        o_im = (p_re[:, 512:] + p_im[:, :512]).reshape(8, 16, 512)
        part[dz, :, :, 0:16, :] = (o_re * w_re - o_im * w_im).reshape(2, 4, 16, 512)
        part[dz, :, :, 16:32, :] = (o_re * w_im + o_im * w_re).reshape(2, 4, 16, 512)
        core_copy(dz).start()

    def multiply(dz, where):
        high, low = xh[:, where], xl[:, where]
        t_high, t_low = th[dz, where, :], tl[dz, where, :]
        return dot(high, t_high) + dot(low, t_high) + dot(high, t_low)

    picks[...] = jnp.zeros_like(picks)
    for other_z in range(4):
        for other_x in range(4):
            value = pick_ref[other_x * 4 + other_z].astype(F32)
            picks[other_z, other_x : other_x + 1, :] = jnp.full((1, 128), value, F32)

    acc = None
    for index in range(PIECES):
        raw_copy(index).wait()
        raw_copy(index + PIECES).wait()
        where = slice(index * width, index * width + width)
        cols = index * width + iota((8, width), 1)
        c_re, c_im = turned(sub * 1031 * cols, 65536)
        c_re, c_im = c_re[0:1], c_im[0:1]
        s_re, s_im = raw[:, where], raw[:, slice(2048 + where.start, 2048 + where.stop)]
        for half, moved in enumerate((s_re * c_re - s_im * c_im, s_re * c_im + s_im * c_re)):
            high, low = split(moved)
            xh[half * 256 : half * 256 + 256, where] = high
            xl[half * 256 : half * 256 + 256, where] = low
        if index == 0:
            for copy in t_copies(order[0]):
                copy.wait()
        more = multiply(order[0], where)
        acc = more if acc is None else acc + more
    pl.semaphore_wait(barrier, 37)
    finish(2, acc)

    def tap_start(step, carry):
        tap_copy(step).start()
        return carry

    lax.fori_loop(1, 32, tap_start, 0)
    tap_out[me] = tap[c * 16 + y * 4 + z]

    def chunk(dz, between):
        for copy in t_copies(dz):
            copy.wait()
        acc = multiply(dz, slice(0, 1024))
        between()
        finish(dz, acc + multiply(dz, slice(1024, 2048)))

    chunk(1, lambda: after_core(2))

    def between_three():
        after_core(1)
        after_y(2)

    chunk(3, between_three)

    def between_four():
        after_core(3)
        after_y(1)

    chunk(0, between_four)
    after_core(0)
    after_y(3)

    def tap_wait(step, carry):
        tap_copy(step).wait_send()
        tap_arrival(step).wait_recv()
        return carry

    lax.fori_loop(1, 32, tap_wait, 0)
    taper = placed_taper(tap_out[...])
    after_y(0)
    for dz in (2, 1, 3):
        z_copy(dz).wait()
    sums = (tot[0] + got_z[0]) + (got_z[1] + got_z[2])

    tapered = sums * jnp.concatenate([taper, taper], 0)
    prod = dot3(tapered, ph[...], pw[...])
    for block in range(8):
        where = slice(block * 128, block * 128 + 128)
        ubuf[block // 2, block % 2] = swapped(prod[:16, where], prod[16:, where])

    def uz_copy(dz):
        to = (z + dz) % 4
        return remote(
            ubuf.at[to], zbuf.at[z], uz_send.at[dz - 1], uz_recv.at[dz - 1], {"facet": to * 4 + y}
        )

    def uz_arrival(dz):
        source = (z - dz + 4) % 4
        return remote(
            ubuf.at[source], zbuf.at[source], uz_send.at[dz - 1], uz_recv.at[dz - 1],
            {"facet": source * 4 + y},
        )

    def uy_copy(index):
        dy, dc = near[index]
        to = (y + dy) % 4
        return remote(
            zbuf.at[:, to // 2], ybuf.at[c, y], uy_send.at[index], uy_recv.at[index],
            {"facet": z * 4 + to, "vis": (c + dc) % 2},
        )

    def uy_arrival(index):
        dy, dc = near[index]
        source = (y - dy + 4) % 4
        return remote(
            zbuf.at[:, 0], ybuf.at[(c + dc) % 2, source], uy_send.at[index], uy_recv.at[index],
            {"facet": z * 4 + source, "vis": (c + dc) % 2},
        )

    for dz in (2, 1, 3):
        uz_copy(dz).start()
    zbuf[z] = ubuf[z]
    for dz in (1, 3, 2):
        uz_arrival(dz).wait_recv()
    for index in range(7):
        uy_copy(index).start()
    ybuf[c, y] = zbuf[:, y // 2]
    for dz in (1, 2, 3):
        uz_copy(dz).wait_send()
    for index in range(7):
        uy_copy(index).wait_send()
        uy_arrival(index).wait_recv()
    cols = ybuf[...].reshape(512, 128).T
    where = pl.ds(pl.multiple_of(((y % 2) * 2 + c) * 256, 256), 256)
    prod = dot3(cols, ph[:, where], pw[:, where])
    for j in range(2):
        where = slice(j * 128, j * 128 + 128)
        own[j] = swapped(prod[:64, where], prod[64:, where])

    def w_copies(dz):
        to = (w + dz) % 4
        device = {"sub": x * 4 + to}
        return (
            remote(own, zpatch.at[dz - 1], w_send.at[dz - 1], w_recv.at[dz - 1], device),
            remote(picks.at[to], zpick.at[dz - 1], p_send.at[dz - 1], p_recv.at[dz - 1], device),
        )

    def x_copy(dx, dz):
        source = (w - dz + 4) % 4
        return remote(
            staged.at[dx - 1, dz], out.at[x * 4 + source], x_send.at[dx - 1, dz],
            x_recv.at[dx - 1, dz], {"sub": (x + dx) % 4 * 4 + w},
        )

    def x_arrival(dx, dz):
        origin = (x - dx + 4) % 4
        source = (w - dz + 4) % 4
        return remote(
            staged.at[dx - 1, dz], out.at[origin * 4 + source], x_send.at[dx - 1, dz],
            x_recv.at[dx - 1, dz], {"sub": origin * 4 + w},
        )

    for dz in (2, 1, 3):
        for copy in w_copies(dz):
            copy.start()
    for dz in (0, 1, 3, 2):
        source = (w - dz + 4) % 4
        if dz:
            for copy in w_copies(dz):
                copy.wait_recv()
            first, second, table = zpatch[dz - 1, 0], zpatch[dz - 1, 1], zpick.at[dz - 1]
        else:
            first, second, table = own[0], own[1], picks.at[w]
        for dx in (2, 1, 3, 0):
            chosen = table[pl.ds((x + dx) % 4, 1), :]
            value = jnp.where(jnp.broadcast_to(chosen, first.shape) > 0.5, second, first)
            if dx:
                staged[dx - 1, dz] = value
                x_copy(dx, dz).start()
            else:
                out[x * 4 + source] = value
    for dz in (1, 2, 3):
        for copy in w_copies(dz):
            copy.wait_send()
    for dz in (0, 1, 3, 2):
        for dx in (1, 3, 2):
            x_copy(dx, dz).wait_send()
            x_arrival(dx, dz).wait_recv()


def shared_patches(strip, tap, pick_row):
    dma = pltpu.SemaphoreType.DMA
    tables = [jnp.asarray(x) for x in column_table() + row_table()]
    ph, pw = (jnp.asarray(x) for x in grid_table())
    far = pl.BlockSpec(memory_space=pl.ANY)
    return pl.pallas_call(
        patch_kernel,
        out_shape=jax.ShapeDtypeStruct((16, 64, 128), F32),
        in_specs=[far] * 3 + [VM] * 5 + [pl.BlockSpec(memory_space=pltpu.SMEM)],
        out_specs=VM,
        scratch_shapes=[
            pltpu.VMEM((256, 4096), F32),
            pltpu.VMEM((512, 2048), BF16),
            pltpu.VMEM((512, 2048), BF16),
            pltpu.VMEM((4, 2048, 256), BF16),
            pltpu.VMEM((4, 2048, 256), BF16),
            pltpu.VMEM((4, 2, 4, 32, 512), F32),
            pltpu.VMEM((4, 4, 32, 512), F32),
            pltpu.VMEM((4, 3, 32, 512), F32),
            pltpu.VMEM((4, 32, 512), F32),
            pltpu.VMEM((3, 32, 512), F32),
            pltpu.VMEM((32, 2, 128), F32),
            pltpu.VMEM((4, 2, 16, 128), F32),
            pltpu.VMEM((4, 2, 16, 128), F32),
            pltpu.VMEM((2, 4, 4, 16, 128), F32),
            pltpu.VMEM((2, 64, 128), F32),
            pltpu.VMEM((4, 8, 128), F32),
            pltpu.VMEM((3, 2, 64, 128), F32),
            pltpu.VMEM((3, 8, 128), F32),
            pltpu.VMEM((3, 4, 64, 128), F32),
            dma((2 * PIECES,)), dma((4, 2)),
            dma((4,)), dma((4,)), dma((4, 3)), dma((4, 3)), dma((3,)), dma((3,)),
            dma((32,)), dma((32,)),
            dma((3,)), dma((3,)), dma((7,)), dma((7,)),
            dma((3,)), dma((3,)), dma((3,)), dma((3,)), dma((3, 4)), dma((3, 4)),
        ],
        compiler_params=pltpu.CompilerParams(
            collective_id=0, has_side_effects=True, vmem_limit_bytes=58 << 20
        ),
    )(strip, *tables, tap, ph, pw, pick_row)


def degrid_kernel(owners, patches, tiles, offsets, eh, el, fh, fl, out):
    low_lane = iota((64, 128), 1) < 64
    cells = iota((64, 1024), 0)

    def one(base, carry):
        patch = patches[owners[base]]
        tile = tiles[base]
        straight = patch * tile
        crossed = patch * pltpu.roll(tile, 64, 1)
        mixed = jnp.where(
            low_lane, straight - pltpu.roll(straight, 64, 1), crossed + pltpu.roll(crossed, 64, 1)
        )
        along = dot3(mixed, eh[...], el[...])
        quad = dot3(along.T, fh[...], fl[...])
        re = quad[:64, :64] - quad[64:, 64:]
        im = quad[:64, 64:] + quad[64:, :64]
        high, low = split(jnp.concatenate([re, im], 0))
        pair = jnp.concatenate([high, low], 1)
        spot = offsets[base]
        hot = jnp.where(cells == spot[0:1], 1.0, 0.0).astype(BF16)
        rows = dot(pair, jnp.concatenate([hot, hot], 0))
        hit = cells == spot[1:2]
        vis_re = jnp.sum(jnp.where(hit, rows[:64], 0.0), 0, keepdims=True)
        vis_im = jnp.sum(jnp.where(hit, rows[64:], 0.0), 0, keepdims=True)
        out[base] = jnp.concatenate([vis_re, vis_im], 0)
        return carry

    lax.fori_loop(0, 8, one, 0, unroll=True)


def degrid(owners, patches, tiles, offsets):
    tables = [jnp.asarray(x) for x in cell_tables()]
    return pl.pallas_call(
        degrid_kernel,
        out_shape=jax.ShapeDtypeStruct((8, 2, 1024), F32),
        in_specs=[pl.BlockSpec(memory_space=pltpu.SMEM)] + [VM] * 7,
        out_specs=VM,
        compiler_params=pltpu.CompilerParams(vmem_limit_bytes=40 << 20),
    )(owners, patches, tiles, offsets, *tables)


def local(facet_strips, taper, send_pick, bl_owner, phase_tiles, cell_offsets):
    tap = taper[0].T.reshape(32, 2, 128)
    patches = shared_patches(facet_strips[0], tap, send_pick[0, 0, 0])
    result = degrid(bl_owner[0, 0, 0], patches, phase_tiles[0, 0, 0], cell_offsets[0, 0, 0])
    return result[None, None, None]


def solution(mesh):
    placed = (
        P("facet", "vis", None),
        P("sub", ("facet", "vis"), None),
        P("facet", "sub", "vis", None),
        P("facet", "sub", "vis", None),
        P("facet", "sub", "vis", None, None, None),
        P("facet", "sub", "vis", None, None, None),
    )
    return jax.shard_map(
        local,
        mesh=mesh,
        in_specs=placed,
        out_specs=P("facet", "sub", "vis", None, None, None),
        check_vma=False,
    )
```

```python
import functools
import math

import jax
import jax.numpy as jnp
import ml_dtypes
import numpy as np
from jax import lax
from jax.experimental import pallas as pl
from jax.experimental.pallas import tpu as pltpu
from jax.sharding import PartitionSpec as P

MESH = pl.DeviceIdType.MESH
F32 = jnp.float32
BF16 = jnp.bfloat16
VM = pl.BlockSpec(memory_space=pltpu.VMEM)
SCALE = 1.0 / math.sqrt(512 * 2048 * 16)


def halves(table):
    high = table.astype(np.float32).astype(ml_dtypes.bfloat16)
    low = (table - high.astype(np.float64)).astype(ml_dtypes.bfloat16)
    return high, low


PIECES = 4
WIDTH = 2048 // PIECES


@functools.lru_cache(None)
def column_table():
    freq = np.arange(512).reshape(2, 4, 4, 16).transpose(2, 0, 1, 3).reshape(4, 1, 128)
    cols = np.arange(2048)[None, :, None]
    angle = (33 * freq * cols % 65536) * (2.0 * np.pi / 65536)
    cos, sin = np.cos(angle), -np.sin(angle)
    top = np.concatenate([cos, sin], 2).reshape(4, PIECES, 1, WIDTH, 256)
    bottom = np.concatenate([-sin, cos], 2).reshape(4, PIECES, 1, WIDTH, 256)
    return halves(np.concatenate([top, bottom], 2).reshape(4, 4096, 256))


@functools.lru_cache(None)
def row_table():
    rows = np.arange(256)[:, None]
    freq = np.arange(512)[None, :]
    angle = (257 * freq * rows % 65536) * (2.0 * np.pi / 65536)
    cos, sin = np.cos(angle), -np.sin(angle)
    top, bottom = np.concatenate([cos, sin], 1), np.concatenate([-sin, cos], 1)
    return halves(np.concatenate([top, bottom], 0))


@functools.lru_cache(None)
def grid_table():
    left = np.arange(512)[:, None]
    right = np.arange(512)[None, :]
    angle = (left * right % 512) * (2.0 * np.pi / 512)
    scale = 1.0 / math.sqrt(512)
    both = np.stack(
        [np.cos(angle).reshape(512, 8, 64) * scale, np.sin(angle).reshape(512, 8, 64) * scale], 2
    )
    return halves(both.reshape(512, 1024))


@functools.lru_cache(None)
def cell_tables():
    left = np.arange(64)[:, None]
    right = np.arange(64)[None, :]
    angle = (left * right % 64) * (2.0 * np.pi / 64)
    cos, sin = np.cos(angle) / 8.0, -np.sin(angle) / 8.0
    square = np.concatenate(
        [np.concatenate([cos, sin], 1), np.concatenate([-sin, cos], 1)], 0
    )
    flat = np.concatenate([cos, sin], 1)
    return halves(square) + halves(flat)


def split(value):
    high = value.astype(BF16)
    return high, (value - high.astype(F32)).astype(BF16)


def dot(left, right):
    return jnp.dot(left, right, preferred_element_type=F32)


def dot_t(left, right):
    return lax.dot_general(left, right, (((1,), (1,)), ((), ())), preferred_element_type=F32)


def dot3(left, right_high, right_low):
    high, low = split(left)
    return dot(high, right_high) + dot(low, right_high) + dot(high, right_low)


def turned(turns, modulus):
    angles = (turns & (modulus - 1)).astype(F32) * (2.0 * math.pi / modulus)
    return jnp.cos(angles), -jnp.sin(angles)


def iota(shape, dim):
    return lax.broadcasted_iota(jnp.int32, shape, dim)


def here():
    facet, sub, core = lax.axis_index("facet"), lax.axis_index("sub"), lax.axis_index("vis")
    return facet // 4, facet % 4, sub // 4, sub % 4, core


def swapped(top, bottom):
    sign = jnp.where(iota(top.shape, 1) < 64, -1.0, 1.0).astype(F32)
    return top + pltpu.roll(bottom, 64, 1) * sign


near = [(dy, dc) for dy in range(4) for dc in range(2) if dy or dc]


def remote(src, dst, send, recv, device):
    return pltpu.make_async_remote_copy(
        src_ref=src, dst_ref=dst, send_sem=send, recv_sem=recv,
        device_id=device, device_id_type=MESH,
    )


def exact(left, chosen):
    high = left.astype(BF16)
    middle, low = split(left - high.astype(F32))
    return dot(high, chosen) + (dot(middle, chosen) + dot(low, chosen))


def ones_where(condition):
    return jnp.where(condition, 1.0, 0.0).astype(BF16)


def cut_taper(rows):
    wide = exact(rows.T, ones_where((iota((16, 256), 1) & 15) == iota((16, 256), 0)))
    hit = (iota((512, 256), 0) & 15) == iota((512, 256), 1) // 16
    return jnp.sum(jnp.where(hit, wide, 0.0).reshape(32, 16, 256), 1)


def placed_taper(blocks):
    values = jnp.concatenate([blocks[:, 0, :], blocks[:, 1, :]], 1).T
    wide = exact(values, ones_where(iota((32, 512), 1) // 16 == iota((32, 512), 0)))
    hit = (iota((256, 512), 0) & 15) == (iota((256, 512), 1) & 15)
    return jnp.sum(jnp.where(hit, wide, 0.0).reshape(16, 16, 512), 1)


def patch_kernel(
    strip, th_hbm, tl_hbm, lh_ref, ll_ref, window, ph, pw, pick_ref, out,
    tap, acc, raw, xh, xl, th, tl, part, got_core, got_y, tot, got_far, got_z, tap_out,
    ubuf, zbuf, ybuf, own, picks, zpatch, zpick, staged,
    raw_sem, t_sem, core_send, core_recv, y_send, y_recv, far_send, far_recv, z_send, z_recv, tap_send, tap_recv,
    uz_send, uz_recv, uy_send, uy_recv, w_send, w_recv, p_send, p_recv, x_send, x_recv,
):
    z, y, x, w, c = here()
    facet, sub, core = lax.axis_index("facet"), lax.axis_index("sub"), c
    me = (z * 4 + y) * 2 + c
    order = (2, 1, 3, 0)

    def piece_copies(index):
        re, im = pl.ds(index * WIDTH, WIDTH), pl.ds(2048 + index * WIDTH, WIDTH)
        rows, at = pl.ds(index * 2 * WIDTH, 2 * WIDTH), (z + order[0]) % 4
        return (
            pltpu.make_async_copy(strip.at[:, re], raw.at[:, re], raw_sem.at[index, 0]),
            pltpu.make_async_copy(strip.at[:, im], raw.at[:, im], raw_sem.at[index, 1]),
            pltpu.make_async_copy(th_hbm.at[at, rows], th.at[order[0], rows], raw_sem.at[index, 2]),
            pltpu.make_async_copy(tl_hbm.at[at, rows], tl.at[order[0], rows], raw_sem.at[index, 3]),
        )

    def t_copies(dz):
        at = (z + dz) % 4
        return (
            pltpu.make_async_copy(th_hbm.at[at], th.at[dz], t_sem.at[dz, 0]),
            pltpu.make_async_copy(tl_hbm.at[at], tl.at[dz], t_sem.at[dz, 1]),
        )

    for index in range(PIECES):
        for copy in piece_copies(index):
            copy.start()
    barrier = pltpu.get_barrier_semaphore()

    def greet(step, carry):
        peer = (me + step) % 32
        pl.semaphore_signal(
            barrier, inc=1, device_id={"facet": peer // 2, "vis": peer % 2}, device_id_type=MESH
        )
        return carry

    lax.fori_loop(1, 32, greet, 0)
    for step in (1, 2, 3):
        pl.semaphore_signal(
            barrier, inc=1, device_id={"sub": x * 4 + (w + step) % 4}, device_id_type=MESH
        )
        pl.semaphore_signal(
            barrier, inc=1, device_id={"sub": (x + step) % 4 * 4 + w}, device_id_type=MESH
        )

    def core_copy(dz):
        return remote(
            part.at[dz, 1 - c], got_core.at[dz], core_send.at[dz], core_recv.at[dz], {"vis": 1 - c}
        )

    def y_copy(dz, dy):
        to = (y + dy) % 4
        return remote(
            part.at[dz, c, to], got_y.at[dz, dy - 1], y_send.at[dz, dy - 1],
            y_recv.at[dz, dy - 1], {"facet": z * 4 + to},
        )

    up_z, down_z = {"facet": (z + 1) % 4 * 4 + y}, {"facet": (z + 3) % 4 * 4 + y}
    first, last = pl.ds(0, 16), pl.ds(16, 16)

    def far_copy(side):
        return remote(
            tot.at[2, last if side else first], got_far.at[side], far_send.at[side],
            far_recv.at[side], down_z if side else up_z,
        )

    def z_copy(side):
        return remote(
            tot.at[1 + 2 * side], got_z.at[side], z_send.at[side], z_recv.at[side],
            down_z if side else up_z,
        )

    def tap_copy(step):
        peer = (me + step) % 32
        block = (peer % 2) * 16 + (peer // 2 % 4) * 4 + peer // 8
        return remote(
            tap.at[block], tap_out.at[me], tap_send.at[step], tap_recv.at[step],
            {"facet": peer // 2, "vis": peer % 2},
        )

    def tap_arrival(step):
        source = (me - step + 32) % 32
        return remote(
            tap.at[0], tap_out.at[source], tap_send.at[step], tap_recv.at[step],
            {"facet": source // 2, "vis": source % 2},
        )

    def after_core(dz):
        core_copy(dz).wait()
        part[dz, c] = part[dz, c] + got_core[dz]
        for dy in (2, 1, 3):
            y_copy(dz, dy).start()

    def after_y(dz):
        for dy in (1, 3, 2):
            y_copy(dz, dy).wait()
        tot[dz] = (part[dz, c, y] + got_y[dz, 0]) + (got_y[dz, 1] + got_y[dz, 2])
        if dz == 2:
            far_copy(0).start()
            far_copy(1).start()

    def after_far(side):
        far_copy(side).wait()
        half, dz = (last, 3) if side else (first, 1)
        tot[dz, half] = tot[dz, half] + got_far[side]
        z_copy(side).start()

    rows = core * 256 + iota((8, 256), 1)
    r_re, r_im = turned(sub * 4099 * rows, 65536)
    r_re, r_im = r_re[0:1], r_im[0:1]
    freq = iota((16, 512), 1)
    other = iota((16, 512), 0)
    turn = facet * ((freq + 5 * other + 6 * sub) & 15) * 16 + freq * core
    w_re, w_im = turned(turn, 256)
    w_re, w_im = (w_re * SCALE)[None], (w_im * SCALE)[None]

    def finish(dz):
        turned_acc = acc[...].T
        a_re, a_im = turned_acc[:128], turned_acc[128:]
        both = jnp.concatenate([a_re * r_re - a_im * r_im, a_re * r_im + a_im * r_re], 1)
        prod = dot3(both, lh_ref[...], ll_ref[...])
        o_re = prod[:, :512].reshape(8, 16, 512)
        o_im = prod[:, 512:].reshape(8, 16, 512)
        part[dz, :, :, 0:16, :] = (o_re * w_re - o_im * w_im).reshape(2, 4, 16, 512)
        part[dz, :, :, 16:32, :] = (o_re * w_im + o_im * w_re).reshape(2, 4, 16, 512)

    def apart(step, value):
        def body(index, carry):
            step(value)
            return carry

        lax.fori_loop(0, 1 + facet // 16, body, 0)

    def multiply(dz, where):
        high, low = xh[:, where], xl[:, where]
        t_high, t_low = th[dz, where, :], tl[dz, where, :]
        return dot(high, t_high) + dot(low, t_high) + dot(high, t_low)

    def prepare(index):
        where = slice(index * WIDTH, index * WIDTH + WIDTH)
        cols = index * WIDTH + iota((8, WIDTH), 1)
        c_re, c_im = turned(sub * 1031 * cols, 65536)
        c_re, c_im = c_re[0:1], c_im[0:1]
        s_re, s_im = raw[:, where], raw[:, slice(2048 + where.start, 2048 + where.stop)]
        for half, moved in enumerate((s_re * c_re - s_im * c_im, s_re * c_im + s_im * c_re)):
            start = (2 * index + half) * WIDTH
            high, low = split(moved)
            xh[:, start : start + WIDTH] = high
            xl[:, start : start + WIDTH] = low

    cut = cut_taper(window[...])
    tap[:, 0, :] = cut[:, :128]
    tap[:, 1, :] = cut[:, 128:]
    picks[...] = jnp.zeros_like(picks)
    for other_z in range(4):
        for other_x in range(4):
            value = pick_ref[other_x * 4 + other_z].astype(F32)
            picks[other_z, other_x : other_x + 1, :] = jnp.full((1, 128), value, F32)

    for index in range(PIECES):
        for copy in piece_copies(index):
            copy.wait()
        if index:
            for copy in t_copies(order[index]):
                copy.start()
        apart(prepare, index)
        def piece(index):
            more = multiply(order[0], slice(2 * index * WIDTH, 2 * (index + 1) * WIDTH))
            acc[...] = more if index == 0 else acc[...] + more
        apart(piece, index)
    apart(finish, 2)
    pl.semaphore_wait(barrier, 37)
    core_copy(2).start()

    def tap_start(step, carry):
        tap_copy(step).start()
        return carry

    lax.fori_loop(1, 32, tap_start, 0)
    tap_out[me] = tap[c * 16 + y * 4 + z]

    def chunk(dz, between):
        for copy in t_copies(dz):
            copy.wait()
        acc[...] = multiply(dz, slice(0, 2048))
        between()
        acc[...] += multiply(dz, slice(2048, 4096))
        apart(finish, dz)
        core_copy(dz).start()

    chunk(1, lambda: after_core(2))

    def between_three():
        after_core(1)
        after_y(2)

    chunk(3, between_three)

    def between_four():
        after_core(3)
        after_y(1)

    chunk(0, between_four)
    after_core(0)
    after_far(0)
    after_y(3)
    after_far(1)

    def tap_wait(step, carry):
        tap_copy(step).wait_send()
        tap_arrival(step).wait_recv()
        return carry

    lax.fori_loop(1, 32, tap_wait, 0)
    taper = placed_taper(tap_out[...])
    after_y(0)
    z_copy(0).wait()
    z_copy(1).wait()
    sums = tot[0] + (got_z[0] + got_z[1])

    tapered = sums * jnp.concatenate([taper, taper], 0)
    prod = dot3(tapered, ph[...], pw[...])
    for block in range(8):
        where = slice(block * 128, block * 128 + 128)
        ubuf[block // 2, block % 2] = swapped(prod[:16, where], prod[16:, where])

    def uz_copy(dz):
        to = (z + dz) % 4
        return remote(
            ubuf.at[to], zbuf.at[z], uz_send.at[dz - 1], uz_recv.at[dz - 1], {"facet": to * 4 + y}
        )

    def uz_arrival(dz):
        source = (z - dz + 4) % 4
        return remote(
            ubuf.at[source], zbuf.at[source], uz_send.at[dz - 1], uz_recv.at[dz - 1],
            {"facet": source * 4 + y},
        )

    def uy_copy(index, dz):
        dy, dc = near[index]
        to = (y + dy) % 4
        source = (z - dz + 4) % 4
        return remote(
            zbuf.at[source, to // 2], ybuf.at[c, y, source], uy_send.at[index, dz],
            uy_recv.at[index, dz], {"facet": z * 4 + to, "vis": (c + dc) % 2},
        )

    def uy_arrival(index, dz):
        dy, dc = near[index]
        origin = (y - dy + 4) % 4
        source = (z - dz + 4) % 4
        return remote(
            zbuf.at[source, 0], ybuf.at[(c + dc) % 2, origin, source], uy_send.at[index, dz],
            uy_recv.at[index, dz], {"facet": z * 4 + origin, "vis": (c + dc) % 2},
        )

    for dz in (2, 1, 3):
        uz_copy(dz).start()
    zbuf[z] = ubuf[z]
    for dz in (0, 1, 3, 2):
        if dz:
            uz_arrival(dz).wait_recv()
        for index in (4, 3, 2, 1, 6, 5, 0):
            uy_copy(index, dz).start()
    ybuf[c, y] = zbuf[:, y // 2]
    for dz in (1, 2, 3):
        uz_copy(dz).wait_send()
    for dz in (0, 1, 3, 2):
        for index in range(7):
            uy_copy(index, dz).wait_send()
            uy_arrival(index, dz).wait_recv()
    cols = ybuf[...].reshape(512, 128).T
    where = pl.ds(pl.multiple_of(((y % 2) * 2 + c) * 256, 256), 256)
    prod = dot3(cols, ph[:, where], pw[:, where])
    for j in range(2):
        where = slice(j * 128, j * 128 + 128)
        own[j] = swapped(prod[:64, where], prod[64:, where])

    def w_copies(dz):
        to = (w + dz) % 4
        device = {"sub": x * 4 + to}
        return (
            remote(own, zpatch.at[dz - 1], w_send.at[dz - 1], w_recv.at[dz - 1], device),
            remote(picks.at[to], zpick.at[dz - 1], p_send.at[dz - 1], p_recv.at[dz - 1], device),
        )

    def x_copy(dx, dz):
        source = (w - dz + 4) % 4
        return remote(
            staged.at[dx - 1, dz], out.at[x * 4 + source], x_send.at[dx - 1, dz],
            x_recv.at[dx - 1, dz], {"sub": (x + dx) % 4 * 4 + w},
        )

    def x_arrival(dx, dz):
        origin = (x - dx + 4) % 4
        source = (w - dz + 4) % 4
        return remote(
            staged.at[dx - 1, dz], out.at[origin * 4 + source], x_send.at[dx - 1, dz],
            x_recv.at[dx - 1, dz], {"sub": origin * 4 + w},
        )

    for dz in (2, 1, 3):
        for copy in w_copies(dz):
            copy.start()
    for dz in (0, 1, 3, 2):
        source = (w - dz + 4) % 4
        if dz:
            for copy in w_copies(dz):
                copy.wait_recv()
            first, second, table = zpatch[dz - 1, 0], zpatch[dz - 1, 1], zpick.at[dz - 1]
        else:
            first, second, table = own[0], own[1], picks.at[w]
        for dx in (2, 1, 3, 0):
            chosen = table[pl.ds((x + dx) % 4, 1), :]
            value = jnp.where(jnp.broadcast_to(chosen, first.shape) > 0.5, second, first)
            if dx:
                staged[dx - 1, dz] = value
                x_copy(dx, dz).start()
            else:
                out[x * 4 + source] = value
    for dz in (1, 2, 3):
        for copy in w_copies(dz):
            copy.wait_send()
    for dz in (0, 1, 3, 2):
        for dx in (1, 3, 2):
            x_copy(dx, dz).wait_send()
            x_arrival(dx, dz).wait_recv()


def shared_patches(strip, window, pick_row):
    dma = pltpu.SemaphoreType.DMA
    tables = [jnp.asarray(x) for x in column_table() + row_table()]
    ph, pw = (jnp.asarray(x) for x in grid_table())
    far = pl.BlockSpec(memory_space=pl.ANY)
    return pl.pallas_call(
        patch_kernel,
        out_shape=jax.ShapeDtypeStruct((16, 64, 128), F32),
        in_specs=[far] * 3 + [VM] * 5 + [pl.BlockSpec(memory_space=pltpu.SMEM)],
        out_specs=VM,
        scratch_shapes=[
            pltpu.VMEM((32, 2, 128), F32),
            pltpu.VMEM((256, 256), F32),
            pltpu.VMEM((256, 4096), F32),
            pltpu.VMEM((256, 4096), BF16),
            pltpu.VMEM((256, 4096), BF16),
            pltpu.VMEM((4, 4096, 256), BF16),
            pltpu.VMEM((4, 4096, 256), BF16),
            pltpu.VMEM((4, 2, 4, 32, 512), F32),
            pltpu.VMEM((4, 4, 32, 512), F32),
            pltpu.VMEM((4, 3, 32, 512), F32),
            pltpu.VMEM((4, 32, 512), F32),
            pltpu.VMEM((2, 16, 512), F32),
            pltpu.VMEM((2, 32, 512), F32),
            pltpu.VMEM((32, 2, 128), F32),
            pltpu.VMEM((4, 2, 16, 128), F32),
            pltpu.VMEM((4, 2, 16, 128), F32),
            pltpu.VMEM((2, 4, 4, 16, 128), F32),
            pltpu.VMEM((2, 64, 128), F32),
            pltpu.VMEM((4, 8, 128), F32),
            pltpu.VMEM((3, 2, 64, 128), F32),
            pltpu.VMEM((3, 8, 128), F32),
            pltpu.VMEM((3, 4, 64, 128), F32),
            dma((PIECES, 4)), dma((4, 2)),
            dma((4,)), dma((4,)), dma((4, 3)), dma((4, 3)), dma((2,)), dma((2,)), dma((2,)), dma((2,)),
            dma((32,)), dma((32,)),
            dma((3,)), dma((3,)), dma((7, 4)), dma((7, 4)),
            dma((3,)), dma((3,)), dma((3,)), dma((3,)), dma((3, 4)), dma((3, 4)),
        ],
        compiler_params=pltpu.CompilerParams(
            collective_id=0, has_side_effects=True, vmem_limit_bytes=58 << 20
        ),
    )(strip, *tables, window, ph, pw, pick_row)


def degrid_kernel(owners, patches, tiles, offsets, eh, el, fh, fl, out):
    low_lane = iota((64, 128), 1) < 64
    cells = iota((64, 1024), 0)
    mixed = []
    for base in range(8):
        patch = patches[owners[base]]
        tile = tiles[base]
        straight = patch * tile
        crossed = patch * pltpu.roll(tile, 64, 1)
        mixed.append(
            jnp.where(
                low_lane,
                straight - pltpu.roll(straight, 64, 1),
                crossed + pltpu.roll(crossed, 64, 1),
            )
        )
    along = dot3(jnp.concatenate(mixed, 0), eh[...], el[...])
    across = jnp.concatenate([along[64 * base : 64 * base + 64].T for base in range(8)], 0)
    quads = dot3(across, fh[...], fl[...])
    for base in range(8):
        quad = quads[128 * base : 128 * base + 128]
        re = quad[:64, :64] - quad[64:, 64:]
        im = quad[:64, 64:] + quad[64:, :64]
        high, low = split(jnp.concatenate([re, im], 0))
        pair = jnp.concatenate([high, low], 1)
        spot = offsets[base]
        hot = ones_where(cells == spot[0:1])
        rows = dot(pair, jnp.concatenate([hot, hot], 0))
        hit = cells == spot[1:2]
        vis_re = jnp.sum(jnp.where(hit, rows[:64], 0.0), 0, keepdims=True)
        vis_im = jnp.sum(jnp.where(hit, rows[64:], 0.0), 0, keepdims=True)
        out[base] = jnp.concatenate([vis_re, vis_im], 0)


def degrid(owners, patches, tiles, offsets):
    tables = [jnp.asarray(x) for x in cell_tables()]
    return pl.pallas_call(
        degrid_kernel,
        out_shape=jax.ShapeDtypeStruct((8, 2, 1024), F32),
        in_specs=[pl.BlockSpec(memory_space=pltpu.SMEM)] + [VM] * 7,
        out_specs=VM,
        compiler_params=pltpu.CompilerParams(vmem_limit_bytes=40 << 20),
    )(owners, patches, tiles, offsets, *tables)


def local(facet_strips, taper, send_pick, bl_owner, phase_tiles, cell_offsets):
    patches = shared_patches(facet_strips[0], taper[0], send_pick[0, 0, 0])
    result = degrid(bl_owner[0, 0, 0], patches, phase_tiles[0, 0, 0], cell_offsets[0, 0, 0])
    return result[None, None, None]


def solution(mesh):
    placed = (
        P("facet", "vis", None),
        P("sub", ("facet", "vis"), None),
        P("facet", "sub", "vis", None),
        P("facet", "sub", "vis", None),
        P("facet", "sub", "vis", None, None, None),
        P("facet", "sub", "vis", None, None, None),
    )
    return jax.shard_map(
        local,
        mesh=mesh,
        in_specs=placed,
        out_specs=P("facet", "sub", "vis", None, None, None),
        check_vma=False,
    )
```

```python
import functools
import math

import jax
import jax.numpy as jnp
import ml_dtypes
import numpy as np
from jax import lax
from jax.experimental import pallas as pl
from jax.experimental.pallas import tpu as pltpu
from jax.sharding import PartitionSpec as P

MESH = pl.DeviceIdType.MESH
F32 = jnp.float32
BF16 = jnp.bfloat16
VM = pl.BlockSpec(memory_space=pltpu.VMEM)
SCALE = 1.0 / math.sqrt(512 * 2048 * 16)


def halves(table):
    high = table.astype(np.float32).astype(ml_dtypes.bfloat16)
    low = (table - high.astype(np.float64)).astype(ml_dtypes.bfloat16)
    return high, low


PIECES = 4
WIDTH = 2048 // PIECES


@functools.lru_cache(None)
def column_table():
    freq = np.arange(512).reshape(2, 4, 4, 16).transpose(2, 0, 1, 3).reshape(4, 1, 128)
    cols = np.arange(2048)[None, :, None]
    angle = (33 * freq * cols % 65536) * (2.0 * np.pi / 65536)
    return halves(np.concatenate([np.cos(angle), -np.sin(angle)], 2))


@functools.lru_cache(None)
def row_table():
    rows = np.arange(256)[:, None]
    freq = np.arange(512)[None, :]
    angle = (257 * freq * rows % 65536) * (2.0 * np.pi / 65536)
    cos, sin = np.cos(angle), -np.sin(angle)
    top, bottom = np.concatenate([cos, sin], 1), np.concatenate([-sin, cos], 1)
    return halves(np.concatenate([top, bottom], 0))


@functools.lru_cache(None)
def grid_table():
    left = np.arange(512)[:, None]
    right = np.arange(512)[None, :]
    angle = (left * right % 512) * (2.0 * np.pi / 512)
    scale = 1.0 / math.sqrt(512)
    both = np.stack(
        [np.cos(angle).reshape(512, 8, 64) * scale, np.sin(angle).reshape(512, 8, 64) * scale], 2
    )
    return halves(both.reshape(512, 1024))


@functools.lru_cache(None)
def cell_tables():
    left = np.arange(64)[:, None]
    right = np.arange(64)[None, :]
    angle = (left * right % 64) * (2.0 * np.pi / 64)
    cos, sin = np.cos(angle) / 8.0, -np.sin(angle) / 8.0
    square = np.concatenate(
        [np.concatenate([cos, sin], 1), np.concatenate([-sin, cos], 1)], 0
    )
    flat = np.concatenate([cos, sin], 1)
    return halves(square) + halves(flat)


def split(value):
    high = value.astype(BF16)
    return high, (value - high.astype(F32)).astype(BF16)


def dot(left, right):
    return jnp.dot(left, right, preferred_element_type=F32)


def dot_t(left, right):
    return lax.dot_general(left, right, (((1,), (1,)), ((), ())), preferred_element_type=F32)


def dot3(left, right_high, right_low):
    high, low = split(left)
    return dot(high, right_high) + dot(low, right_high) + dot(high, right_low)


def turned(turns, modulus):
    angles = (turns & (modulus - 1)).astype(F32) * (2.0 * math.pi / modulus)
    return jnp.cos(angles), -jnp.sin(angles)


def iota(shape, dim):
    return lax.broadcasted_iota(jnp.int32, shape, dim)


def here():
    facet, sub, core = lax.axis_index("facet"), lax.axis_index("sub"), lax.axis_index("vis")
    return facet // 4, facet % 4, sub // 4, sub % 4, core


def swapped(top, bottom):
    sign = jnp.where(iota(top.shape, 1) < 64, -1.0, 1.0).astype(F32)
    return top + pltpu.roll(bottom, 64, 1) * sign


near = [(dy, dc) for dy in range(4) for dc in range(2) if dy or dc]


def remote(src, dst, send, recv, device):
    return pltpu.make_async_remote_copy(
        src_ref=src, dst_ref=dst, send_sem=send, recv_sem=recv,
        device_id=device, device_id_type=MESH,
    )


def exact(left, chosen):
    high = left.astype(BF16)
    middle, low = split(left - high.astype(F32))
    return dot(high, chosen) + (dot(middle, chosen) + dot(low, chosen))


def ones_where(condition):
    return jnp.where(condition, 1.0, 0.0).astype(BF16)


def cut_taper(rows):
    wide = exact(rows.T, ones_where((iota((16, 256), 1) & 15) == iota((16, 256), 0)))
    hit = (iota((512, 256), 0) & 15) == iota((512, 256), 1) // 16
    return jnp.sum(jnp.where(hit, wide, 0.0).reshape(32, 16, 256), 1)


def placed_taper(blocks):
    values = jnp.concatenate([blocks[:, 0, :], blocks[:, 1, :]], 1).T
    wide = exact(values, ones_where(iota((32, 512), 1) // 16 == iota((32, 512), 0)))
    hit = (iota((256, 512), 0) & 15) == (iota((256, 512), 1) & 15)
    return jnp.sum(jnp.where(hit, wide, 0.0).reshape(16, 16, 512), 1)


def degrid(owners, patches, tiles, offsets, hots, eh, el, fh, fl, out):
    low_lane = iota((64, 128), 1) < 64
    cells = iota((64, 1024), 0)
    mixed = []
    for base in range(8):
        patch = patches[owners[base]]
        tile = tiles[base]
        straight = patch * tile
        crossed = patch * pltpu.roll(tile, 64, 1)
        mixed.append(
            jnp.where(
                low_lane,
                straight - pltpu.roll(straight, 64, 1),
                crossed + pltpu.roll(crossed, 64, 1),
            )
        )
    along = dot3(jnp.concatenate(mixed, 0), eh[...], el[...])
    across = jnp.concatenate([along[64 * base : 64 * base + 64].T for base in range(8)], 0)
    quads = dot3(across, fh[...], fl[...])
    for base in range(8):
        quad = quads[128 * base : 128 * base + 128]
        re = quad[:64, :64] - quad[64:, 64:]
        im = quad[:64, 64:] + quad[64:, :64]
        high, low = split(jnp.concatenate([re, im], 0))
        pair = jnp.concatenate([high, low], 1)
        spot = offsets[base]
        hot = hots[base]
        rows = dot(pair, jnp.concatenate([hot, hot], 0))
        hit = cells == spot[1:2]
        vis_re = jnp.sum(jnp.where(hit, rows[:64], 0.0), 0, keepdims=True)
        vis_im = jnp.sum(jnp.where(hit, rows[64:], 0.0), 0, keepdims=True)
        out[base] = jnp.concatenate([vis_re, vis_im], 0)


def patch_kernel(
    strip, th_hbm, tl_hbm, window, pick_ref, owners,
    lh_hbm, ll_hbm, ph_hbm, pw_hbm, tiles_hbm, offsets_hbm, eh_hbm, el_hbm, fh_hbm, fl_hbm, vis,
    lh_ref, ll_ref, ph, pw, tiles, offsets, eh, el, fh, fl, out, hot,
    tap, acc, raw, xh, xl, th, tl, part, got_core, got_y, tot, got_far, got_z, tap_out,
    ubuf, zbuf, ybuf, own, picks, zpatch, zpick, staged,
    late_sem, raw_sem, t_sem, core_send, core_recv, y_send, y_recv, far_send, far_recv, z_send, z_recv, tap_send, tap_recv,
    uz_send, uz_recv, uy_send, uy_recv, w_send, w_recv, p_send, p_recv, x_send, x_recv,
):
    z, y, x, w, c = here()
    facet, sub, core = lax.axis_index("facet"), lax.axis_index("sub"), c
    me = (z * 4 + y) * 2 + c
    order = (2, 1, 3, 0)

    def piece_copies(index):
        re, im = pl.ds(index * WIDTH, WIDTH), pl.ds(2048 + index * WIDTH, WIDTH)
        rows, at = re, (z + order[0]) % 4
        return (
            pltpu.make_async_copy(strip.at[:, re], raw.at[:, re], raw_sem.at[index, 0]),
            pltpu.make_async_copy(strip.at[:, im], raw.at[:, im], raw_sem.at[index, 1]),
            pltpu.make_async_copy(th_hbm.at[at, rows], th.at[order[0], rows], raw_sem.at[index, 2]),
            pltpu.make_async_copy(tl_hbm.at[at, rows], tl.at[order[0], rows], raw_sem.at[index, 3]),
        )

    def t_copies(dz):
        at = (z + dz) % 4
        return (
            pltpu.make_async_copy(th_hbm.at[at], th.at[dz], t_sem.at[dz, 0]),
            pltpu.make_async_copy(tl_hbm.at[at], tl.at[dz], t_sem.at[dz, 1]),
        )

    for index in range(PIECES):
        for copy in piece_copies(index):
            copy.start()
    late = [
        pltpu.make_async_copy(source, target, late_sem.at[index])
        for index, (source, target) in enumerate(
            (
                (lh_hbm, lh_ref), (ll_hbm, ll_ref), (ph_hbm, ph), (pw_hbm, pw),
                (tiles_hbm, tiles), (offsets_hbm, offsets),
                (eh_hbm, eh), (el_hbm, el), (fh_hbm, fh), (fl_hbm, fl),
            )
        )
    ]
    for copy in late[:2]:
        copy.start()

    barrier = pltpu.get_barrier_semaphore()

    def greet(step, carry):
        peer = (me + step) % 32
        pl.semaphore_signal(
            barrier, inc=1, device_id={"facet": peer // 2, "vis": peer % 2}, device_id_type=MESH
        )
        return carry

    lax.fori_loop(1, 32, greet, 0)
    for step in (1, 2, 3):
        pl.semaphore_signal(
            barrier, inc=1, device_id={"sub": x * 4 + (w + step) % 4}, device_id_type=MESH
        )
        pl.semaphore_signal(
            barrier, inc=1, device_id={"sub": (x + step) % 4 * 4 + w}, device_id_type=MESH
        )

    def core_copy(dz):
        return remote(
            part.at[dz, 1 - c], got_core.at[dz], core_send.at[dz], core_recv.at[dz], {"vis": 1 - c}
        )

    def y_copy(dz, dy):
        to = (y + dy) % 4
        return remote(
            part.at[dz, c, to], got_y.at[dz, dy - 1], y_send.at[dz, dy - 1],
            y_recv.at[dz, dy - 1], {"facet": z * 4 + to},
        )

    up_z, down_z = {"facet": (z + 1) % 4 * 4 + y}, {"facet": (z + 3) % 4 * 4 + y}
    first, last = pl.ds(0, 16), pl.ds(16, 16)

    def far_copy(side):
        return remote(
            tot.at[2, last if side else first], got_far.at[side], far_send.at[side],
            far_recv.at[side], down_z if side else up_z,
        )

    def z_copy(side):
        return remote(
            tot.at[1 + 2 * side], got_z.at[side], z_send.at[side], z_recv.at[side],
            down_z if side else up_z,
        )

    def tap_copy(step):
        peer = (me + step) % 32
        block = (peer % 2) * 16 + (peer // 2 % 4) * 4 + peer // 8
        return remote(
            tap.at[block], tap_out.at[me], tap_send.at[step], tap_recv.at[step],
            {"facet": peer // 2, "vis": peer % 2},
        )

    def tap_arrival(step):
        source = (me - step + 32) % 32
        return remote(
            tap.at[0], tap_out.at[source], tap_send.at[step], tap_recv.at[step],
            {"facet": source // 2, "vis": source % 2},
        )

    def after_core(dz):
        core_copy(dz).wait()
        part[dz, c] = part[dz, c] + got_core[dz]
        for dy in (2, 1, 3):
            y_copy(dz, dy).start()

    def after_y(dz):
        for dy in (1, 3, 2):
            y_copy(dz, dy).wait()
        tot[dz] = (part[dz, c, y] + got_y[dz, 0]) + (got_y[dz, 1] + got_y[dz, 2])
        if dz == 2:
            far_copy(0).start()
            far_copy(1).start()

    def after_far(side):
        far_copy(side).wait()
        half, dz = (last, 3) if side else (first, 1)
        tot[dz, half] = tot[dz, half] + got_far[side]
        z_copy(side).start()

    rows = core * 256 + iota((8, 256), 1)
    r_re, r_im = turned(sub * 4099 * rows, 65536)
    r_re, r_im = r_re[0:1], r_im[0:1]
    freq = iota((16, 512), 1)
    other = iota((16, 512), 0)
    turn = facet * ((freq + 5 * other + 6 * sub) & 15) * 16 + freq * core
    w_re, w_im = turned(turn, 256)
    w_re, w_im = (w_re * SCALE)[None], (w_im * SCALE)[None]

    def finish(dz):
        a_re = (acc[:256, :128] - acc[256:, 128:]).T
        a_im = (acc[:256, 128:] + acc[256:, :128]).T
        both = jnp.concatenate([a_re * r_re - a_im * r_im, a_re * r_im + a_im * r_re], 1)
        prod = dot3(both, lh_ref[...], ll_ref[...])
        o_re = prod[:, :512].reshape(8, 16, 512)
        o_im = prod[:, 512:].reshape(8, 16, 512)
        part[dz, :, :, 0:16, :] = (o_re * w_re - o_im * w_im).reshape(2, 4, 16, 512)
        part[dz, :, :, 16:32, :] = (o_re * w_im + o_im * w_re).reshape(2, 4, 16, 512)

    def apart(step, value):
        def body(index, carry):
            step(value)
            return carry

        lax.fori_loop(0, 1 + facet // 16, body, 0)

    def multiply(dz, where):
        high, low = xh[:, where], xl[:, where]
        t_high, t_low = th[dz, where, :], tl[dz, where, :]
        return dot(high, t_high) + dot(low, t_high) + dot(high, t_low)

    def prepare(index):
        where = slice(index * WIDTH, index * WIDTH + WIDTH)
        cols = index * WIDTH + iota((8, WIDTH), 1)
        c_re, c_im = turned(sub * 1031 * cols, 65536)
        c_re, c_im = c_re[0:1], c_im[0:1]
        s_re, s_im = raw[:, where], raw[:, slice(2048 + where.start, 2048 + where.stop)]
        for half, moved in enumerate((s_re * c_re - s_im * c_im, s_re * c_im + s_im * c_re)):
            high, low = split(moved)
            xh[half * 256 : half * 256 + 256, where] = high
            xl[half * 256 : half * 256 + 256, where] = low

    cut = cut_taper(window[...])
    tap[:, 0, :] = cut[:, :128]
    tap[:, 1, :] = cut[:, 128:]
    picks[...] = jnp.zeros_like(picks)
    for other_z in range(4):
        for other_x in range(4):
            value = pick_ref[other_x * 4 + other_z].astype(F32)
            picks[other_z, other_x : other_x + 1, :] = jnp.full((1, 128), value, F32)

    for index in range(PIECES):
        for copy in piece_copies(index):
            copy.wait()
        if index:
            for copy in t_copies(order[index]):
                copy.start()
        apart(prepare, index)
        def piece(index):
            more = multiply(order[0], slice(index * WIDTH, (index + 1) * WIDTH))
            acc[...] = more if index == 0 else acc[...] + more
        apart(piece, index)
    for copy in late[:2]:
        copy.wait()
    for copy in late[2:]:
        copy.start()
    apart(finish, 2)
    pl.semaphore_wait(barrier, 37)
    core_copy(2).start()

    def tap_start(step, carry):
        tap_copy(step).start()
        return carry

    lax.fori_loop(1, 32, tap_start, 0)
    tap_out[me] = tap[c * 16 + y * 4 + z]

    def chunk(dz, between):
        for copy in t_copies(dz):
            copy.wait()
        acc[...] = multiply(dz, slice(0, 1024))
        between()
        acc[...] += multiply(dz, slice(1024, 2048))
        apart(finish, dz)
        core_copy(dz).start()

    chunk(1, lambda: after_core(2))

    def between_three():
        after_core(1)
        after_y(2)

    chunk(3, between_three)

    def between_four():
        after_core(3)
        after_y(1)

    chunk(0, between_four)
    after_core(0)
    after_far(0)
    after_y(3)
    after_far(1)

    def tap_wait(step, carry):
        tap_copy(step).wait_send()
        tap_arrival(step).wait_recv()
        return carry

    lax.fori_loop(1, 32, tap_wait, 0)
    taper = placed_taper(tap_out[...])
    after_y(0)
    z_copy(0).wait()
    z_copy(1).wait()
    sums = tot[0] + (got_z[0] + got_z[1])

    for copy in late[2:]:
        copy.wait()

    tapered = sums * jnp.concatenate([taper, taper], 0)
    prod = dot3(tapered, ph[...], pw[...])
    for block in range(8):
        where = slice(block * 128, block * 128 + 128)
        ubuf[block // 2, block % 2] = swapped(prod[:16, where], prod[16:, where])

    def uz_copy(dz):
        to = (z + dz) % 4
        return remote(
            ubuf.at[to], zbuf.at[z], uz_send.at[dz - 1], uz_recv.at[dz - 1], {"facet": to * 4 + y}
        )

    def uz_arrival(dz):
        source = (z - dz + 4) % 4
        return remote(
            ubuf.at[source], zbuf.at[source], uz_send.at[dz - 1], uz_recv.at[dz - 1],
            {"facet": source * 4 + y},
        )

    def uy_copy(index, dz):
        dy, dc = near[index]
        to = (y + dy) % 4
        source = (z - dz + 4) % 4
        return remote(
            zbuf.at[source, to // 2], ybuf.at[c, y, source], uy_send.at[index, dz],
            uy_recv.at[index, dz], {"facet": z * 4 + to, "vis": (c + dc) % 2},
        )

    def uy_arrival(index, dz):
        dy, dc = near[index]
        origin = (y - dy + 4) % 4
        source = (z - dz + 4) % 4
        return remote(
            zbuf.at[source, 0], ybuf.at[(c + dc) % 2, origin, source], uy_send.at[index, dz],
            uy_recv.at[index, dz], {"facet": z * 4 + origin, "vis": (c + dc) % 2},
        )

    for dz in (2, 1, 3):
        uz_copy(dz).start()
    zbuf[z] = ubuf[z]
    for dz in (0, 1, 3, 2):
        if dz:
            uz_arrival(dz).wait_recv()
        for index in (4, 3, 2, 1, 6, 5, 0):
            uy_copy(index, dz).start()
    ybuf[c, y] = zbuf[:, y // 2]
    for dz in (1, 2, 3):
        uz_copy(dz).wait_send()
    for dz in (0, 1, 3, 2):
        for index in range(7):
            uy_copy(index, dz).wait_send()
            uy_arrival(index, dz).wait_recv()
    cols = ybuf[...].reshape(512, 128).T
    where = pl.ds(pl.multiple_of(((y % 2) * 2 + c) * 256, 256), 256)
    prod = dot3(cols, ph[:, where], pw[:, where])
    for j in range(2):
        where = slice(j * 128, j * 128 + 128)
        own[j] = swapped(prod[:64, where], prod[64:, where])

    def w_copies(dz):
        to = (w + dz) % 4
        device = {"sub": x * 4 + to}
        return (
            remote(own, zpatch.at[dz - 1], w_send.at[dz - 1], w_recv.at[dz - 1], device),
            remote(picks.at[to], zpick.at[dz - 1], p_send.at[dz - 1], p_recv.at[dz - 1], device),
        )

    def x_copy(dx, dz):
        source = (w - dz + 4) % 4
        return remote(
            staged.at[dx - 1, dz], out.at[x * 4 + source], x_send.at[dx - 1, dz],
            x_recv.at[dx - 1, dz], {"sub": (x + dx) % 4 * 4 + w},
        )

    def x_arrival(dx, dz):
        origin = (x - dx + 4) % 4
        source = (w - dz + 4) % 4
        return remote(
            staged.at[dx - 1, dz], out.at[origin * 4 + source], x_send.at[dx - 1, dz],
            x_recv.at[dx - 1, dz], {"sub": origin * 4 + w},
        )

    cells = iota((64, 1024), 0)

    def mark(unused):
        for base in range(8):
            hot[base] = ones_where(cells == offsets[base, 0:1, :])

    for dz in (2, 1, 3):
        for copy in w_copies(dz):
            copy.start()
    for dz in (0, 1, 3, 2):
        source = (w - dz + 4) % 4
        if dz:
            for copy in w_copies(dz):
                copy.wait_recv()
            first, second, table = zpatch[dz - 1, 0], zpatch[dz - 1, 1], zpick.at[dz - 1]
        else:
            first, second, table = own[0], own[1], picks.at[w]
        for dx in (2, 1, 3, 0):
            chosen = table[pl.ds((x + dx) % 4, 1), :]
            value = jnp.where(jnp.broadcast_to(chosen, first.shape) > 0.5, second, first)
            if dx:
                staged[dx - 1, dz] = value
                x_copy(dx, dz).start()
            else:
                out[x * 4 + source] = value
        if dz == 0:
            apart(mark, 0)
    for dz in (1, 2, 3):
        for copy in w_copies(dz):
            copy.wait_send()
    for dz in (0, 1, 3, 2):
        for dx in (1, 3, 2):
            x_copy(dx, dz).wait_send()
            x_arrival(dx, dz).wait_recv()
    degrid(owners, out, tiles, offsets, hot, eh, el, fh, fl, vis)


def predicted(strip, window, pick_row, owners, tiles, offsets):
    dma = pltpu.SemaphoreType.DMA
    column = [jnp.asarray(x) for x in column_table()]
    rest = [jnp.asarray(x) for x in row_table() + grid_table()]
    cells = [jnp.asarray(x) for x in cell_tables()]
    far = pl.BlockSpec(memory_space=pl.ANY)
    small = pl.BlockSpec(memory_space=pltpu.SMEM)
    return pl.pallas_call(
        patch_kernel,
        out_shape=jax.ShapeDtypeStruct((8, 2, 1024), F32),
        in_specs=[far] * 3 + [VM, small, small] + [far] * 10,
        out_specs=VM,
        scratch_shapes=[
            pltpu.VMEM((512, 1024), BF16),
            pltpu.VMEM((512, 1024), BF16),
            pltpu.VMEM((512, 1024), BF16),
            pltpu.VMEM((512, 1024), BF16),
            pltpu.VMEM((8, 64, 128), F32),
            pltpu.VMEM((8, 2, 1024), jnp.int32),
            pltpu.VMEM((128, 128), BF16),
            pltpu.VMEM((128, 128), BF16),
            pltpu.VMEM((64, 128), BF16),
            pltpu.VMEM((64, 128), BF16),
            pltpu.VMEM((16, 64, 128), F32),
            pltpu.VMEM((8, 64, 1024), BF16),
            pltpu.VMEM((32, 2, 128), F32),
            pltpu.VMEM((512, 256), F32),
            pltpu.VMEM((256, 4096), F32),
            pltpu.VMEM((512, 2048), BF16),
            pltpu.VMEM((512, 2048), BF16),
            pltpu.VMEM((4, 2048, 256), BF16),
            pltpu.VMEM((4, 2048, 256), BF16),
            pltpu.VMEM((4, 2, 4, 32, 512), F32),
            pltpu.VMEM((4, 4, 32, 512), F32),
            pltpu.VMEM((4, 3, 32, 512), F32),
            pltpu.VMEM((4, 32, 512), F32),
            pltpu.VMEM((2, 16, 512), F32),
            pltpu.VMEM((2, 32, 512), F32),
            pltpu.VMEM((32, 2, 128), F32),
            pltpu.VMEM((4, 2, 16, 128), F32),
            pltpu.VMEM((4, 2, 16, 128), F32),
            pltpu.VMEM((2, 4, 4, 16, 128), F32),
            pltpu.VMEM((2, 64, 128), F32),
            pltpu.VMEM((4, 8, 128), F32),
            pltpu.VMEM((3, 2, 64, 128), F32),
            pltpu.VMEM((3, 8, 128), F32),
            pltpu.VMEM((3, 4, 64, 128), F32),
            dma((10,)), dma((PIECES, 4)), dma((4, 2)),
            dma((4,)), dma((4,)), dma((4, 3)), dma((4, 3)), dma((2,)), dma((2,)), dma((2,)), dma((2,)),
            dma((32,)), dma((32,)),
            dma((3,)), dma((3,)), dma((7, 4)), dma((7, 4)),
            dma((3,)), dma((3,)), dma((3,)), dma((3,)), dma((3, 4)), dma((3, 4)),
        ],
        compiler_params=pltpu.CompilerParams(
            collective_id=0, has_side_effects=True, vmem_limit_bytes=58 << 20
        ),
    )(strip, *column, window, pick_row, owners, *rest, tiles, offsets, *cells)


def local(facet_strips, taper, send_pick, bl_owner, phase_tiles, cell_offsets):
    result = predicted(
        facet_strips[0], taper[0], send_pick[0, 0, 0], bl_owner[0, 0, 0],
        phase_tiles[0, 0, 0], cell_offsets[0, 0, 0],
    )
    return result[None, None, None]


def solution(mesh):
    placed = (
        P("facet", "vis", None),
        P("sub", ("facet", "vis"), None),
        P("facet", "sub", "vis", None),
        P("facet", "sub", "vis", None),
        P("facet", "sub", "vis", None, None, None),
        P("facet", "sub", "vis", None, None, None),
    )
    return jax.shard_map(
        local,
        mesh=mesh,
        in_specs=placed,
        out_specs=P("facet", "sub", "vis", None, None, None),
        check_vma=False,
    )
```

```python
import functools
import math

import jax
import jax.numpy as jnp
import ml_dtypes
import numpy as np
from jax import lax
from jax.experimental import pallas as pl
from jax.experimental.pallas import tpu as pltpu
from jax.sharding import PartitionSpec as P

MESH = pl.DeviceIdType.MESH
F32 = jnp.float32
BF16 = jnp.bfloat16
VM = pl.BlockSpec(memory_space=pltpu.VMEM)
SCALE = 1.0 / math.sqrt(512 * 2048 * 16)


def halves(table):
    high = table.astype(np.float32).astype(ml_dtypes.bfloat16)
    low = (table - high.astype(np.float64)).astype(ml_dtypes.bfloat16)
    return high, low


PIECES = 4
WIDTH = 2048 // PIECES


@functools.lru_cache(None)
def column_table():
    freq = np.arange(512).reshape(2, 4, 4, 16).transpose(2, 0, 1, 3).reshape(4, 1, 128)
    cols = np.arange(2048)[None, :, None]
    angle = (33 * freq * cols % 65536) * (2.0 * np.pi / 65536)
    return halves(np.concatenate([np.cos(angle), -np.sin(angle)], 2))


@functools.lru_cache(None)
def row_table():
    rows = np.arange(256)[:, None]
    freq = np.arange(512)[None, :]
    angle = (257 * freq * rows % 65536) * (2.0 * np.pi / 65536)
    cos, sin = np.cos(angle), -np.sin(angle)
    top, bottom = np.concatenate([cos, sin], 1), np.concatenate([-sin, cos], 1)
    return halves(np.concatenate([top, bottom], 0))


@functools.lru_cache(None)
def grid_table():
    left = np.arange(512)[:, None]
    right = np.arange(512)[None, :]
    angle = (left * right % 512) * (2.0 * np.pi / 512)
    scale = 1.0 / math.sqrt(512)
    both = np.stack(
        [np.cos(angle).reshape(512, 8, 64) * scale, np.sin(angle).reshape(512, 8, 64) * scale], 2
    )
    return halves(both.reshape(512, 1024))


@functools.lru_cache(None)
def cell_tables():
    left = np.arange(64)[:, None]
    right = np.arange(64)[None, :]
    angle = (left * right % 64) * (2.0 * np.pi / 64)
    cos, sin = np.cos(angle) / 8.0, -np.sin(angle) / 8.0
    square = np.concatenate(
        [np.concatenate([cos, sin], 1), np.concatenate([-sin, cos], 1)], 0
    )
    flat = np.concatenate([cos, sin], 1)
    return halves(square) + halves(flat)


def split(value):
    high = value.astype(BF16)
    return high, (value - high.astype(F32)).astype(BF16)


def dot(left, right):
    return jnp.dot(left, right, preferred_element_type=F32)


def dot_t(left, right):
    return lax.dot_general(left, right, (((1,), (1,)), ((), ())), preferred_element_type=F32)


def dot3(left, right_high, right_low):
    high, low = split(left)
    return dot(high, right_high) + dot(low, right_high) + dot(high, right_low)


def turned(turns, modulus):
    angles = (turns & (modulus - 1)).astype(F32) * (2.0 * math.pi / modulus)
    return jnp.cos(angles), -jnp.sin(angles)


def iota(shape, dim):
    return lax.broadcasted_iota(jnp.int32, shape, dim)


def here():
    facet, sub, core = lax.axis_index("facet"), lax.axis_index("sub"), lax.axis_index("vis")
    return facet // 4, facet % 4, sub // 4, sub % 4, core


def swapped(top, bottom):
    sign = jnp.where(iota(top.shape, 1) < 64, -1.0, 1.0).astype(F32)
    return top + pltpu.roll(bottom, 64, 1) * sign


near = [(dy, dc) for dy in range(4) for dc in range(2) if dy or dc]


def remote(src, dst, send, recv, device):
    return pltpu.make_async_remote_copy(
        src_ref=src, dst_ref=dst, send_sem=send, recv_sem=recv,
        device_id=device, device_id_type=MESH,
    )


def exact(left, chosen):
    high = left.astype(BF16)
    middle, low = split(left - high.astype(F32))
    return dot(high, chosen) + (dot(middle, chosen) + dot(low, chosen))


def ones_where(condition):
    return jnp.where(condition, 1.0, 0.0).astype(BF16)


def cut_taper(rows):
    wide = exact(rows.T, ones_where((iota((16, 256), 1) & 15) == iota((16, 256), 0)))
    hit = (iota((512, 256), 0) & 15) == iota((512, 256), 1) // 16
    return jnp.sum(jnp.where(hit, wide, 0.0).reshape(32, 16, 256), 1)


def placed_taper(blocks):
    values = jnp.concatenate([blocks[:, 0, :], blocks[:, 1, :]], 1).T
    wide = exact(values, ones_where(iota((32, 512), 1) // 16 == iota((32, 512), 0)))
    hit = (iota((256, 512), 0) & 15) == (iota((256, 512), 1) & 15)
    return jnp.sum(jnp.where(hit, wide, 0.0).reshape(16, 16, 512), 1)


def degrid(owners, patches, tiles, offsets, hots, eh, el, fh, fl, out):
    low_lane = iota((64, 128), 1) < 64
    cells = iota((64, 1024), 0)
    mixed = []
    for base in range(8):
        patch = patches[owners[base]]
        tile = tiles[base]
        straight = patch * tile
        crossed = patch * pltpu.roll(tile, 64, 1)
        mixed.append(
            jnp.where(
                low_lane,
                straight - pltpu.roll(straight, 64, 1),
                crossed + pltpu.roll(crossed, 64, 1),
            )
        )
    along = dot3(jnp.concatenate(mixed, 0), eh[...], el[...])
    across = jnp.concatenate([along[64 * base : 64 * base + 64].T for base in range(8)], 0)
    quads = dot3(across, fh[...], fl[...])
    for base in range(8):
        quad = quads[128 * base : 128 * base + 128]
        re = quad[:64, :64] - quad[64:, 64:]
        im = quad[:64, 64:] + quad[64:, :64]
        high, low = split(jnp.concatenate([re, im], 0))
        pair = jnp.concatenate([high, low], 1)
        spot = offsets[base]
        hot = hots[base]
        rows = dot(pair, jnp.concatenate([hot, hot], 0))
        hit = cells == spot[1:2]
        vis_re = jnp.sum(jnp.where(hit, rows[:64], 0.0), 0, keepdims=True)
        vis_im = jnp.sum(jnp.where(hit, rows[64:], 0.0), 0, keepdims=True)
        out[base] = jnp.concatenate([vis_re, vis_im], 0)


def patch_kernel(
    strip, th_hbm, tl_hbm, window, pick_ref, owners,
    lh_hbm, ll_hbm, ph_hbm, pw_hbm, tiles_hbm, offsets_hbm, eh_hbm, el_hbm, fh_hbm, fl_hbm, vis,
    lh_ref, ll_ref, ph, pw, tiles, offsets, eh, el, fh, fl, out, hot,
    tap, acc, raw, xh, xl, th, tl, part, got_core, got_y, tot, got_far, got_z, tap_out,
    ubuf, zbuf, ybuf, own, picks, zpatch, zpick, staged,
    late_sem, raw_sem, t_sem, core_send, core_recv, y_send, y_recv, far_send, far_recv, z_send, z_recv, tap_send, tap_recv,
    uz_send, uz_recv, uy_send, uy_recv, w_send, w_recv, p_send, p_recv, x_send, x_recv,
):
    z, y, x, w, c = here()
    facet, sub, core = lax.axis_index("facet"), lax.axis_index("sub"), c
    me = (z * 4 + y) * 2 + c
    order = (2, 1, 3, 0)

    def piece_copies(index):
        re, im = pl.ds(index * WIDTH, WIDTH), pl.ds(2048 + index * WIDTH, WIDTH)
        rows, at = re, (z + order[0]) % 4
        return (
            pltpu.make_async_copy(strip.at[:, re], raw.at[:, re], raw_sem.at[index, 0]),
            pltpu.make_async_copy(strip.at[:, im], raw.at[:, im], raw_sem.at[index, 1]),
            pltpu.make_async_copy(th_hbm.at[at, rows], th.at[order[0], rows], raw_sem.at[index, 2]),
            pltpu.make_async_copy(tl_hbm.at[at, rows], tl.at[order[0], rows], raw_sem.at[index, 3]),
        )

    def t_copies(dz):
        at = (z + dz) % 4
        return (
            pltpu.make_async_copy(th_hbm.at[at], th.at[dz], t_sem.at[dz, 0]),
            pltpu.make_async_copy(tl_hbm.at[at], tl.at[dz], t_sem.at[dz, 1]),
        )

    for index in range(PIECES):
        for copy in piece_copies(index):
            copy.start()
    late = [
        pltpu.make_async_copy(source, target, late_sem.at[index])
        for index, (source, target) in enumerate(
            (
                (lh_hbm, lh_ref), (ll_hbm, ll_ref), (ph_hbm, ph), (pw_hbm, pw),
                (tiles_hbm, tiles), (offsets_hbm, offsets),
                (eh_hbm, eh), (el_hbm, el), (fh_hbm, fh), (fl_hbm, fl),
            )
        )
    ]
    for copy in late[:2]:
        copy.start()

    barrier = pltpu.get_barrier_semaphore()

    def greet(step, carry):
        peer = (me + step) % 32
        pl.semaphore_signal(
            barrier, inc=1, device_id={"facet": peer // 2, "vis": peer % 2}, device_id_type=MESH
        )
        return carry

    lax.fori_loop(1, 32, greet, 0)
    for step in (1, 2, 3):
        pl.semaphore_signal(
            barrier, inc=1, device_id={"sub": x * 4 + (w + step) % 4}, device_id_type=MESH
        )
        pl.semaphore_signal(
            barrier, inc=1, device_id={"sub": (x + step) % 4 * 4 + w}, device_id_type=MESH
        )

    def core_copy(dz):
        return remote(
            part.at[dz, 1 - c], got_core.at[dz], core_send.at[dz], core_recv.at[dz], {"vis": 1 - c}
        )

    def y_copy(dz, dy):
        to = (y + dy) % 4
        return remote(
            part.at[dz, c, to], got_y.at[dz, dy - 1], y_send.at[dz, dy - 1],
            y_recv.at[dz, dy - 1], {"facet": z * 4 + to},
        )

    up_z, down_z = {"facet": (z + 1) % 4 * 4 + y}, {"facet": (z + 3) % 4 * 4 + y}
    first, last = pl.ds(0, 16), pl.ds(16, 16)

    def far_copy(side):
        return remote(
            tot.at[2, last if side else first], got_far.at[side], far_send.at[side],
            far_recv.at[side], down_z if side else up_z,
        )

    def z_copy(side):
        return remote(
            tot.at[1 + 2 * side], got_z.at[side], z_send.at[side], z_recv.at[side],
            down_z if side else up_z,
        )

    def tap_copy(step):
        peer = (me + step) % 32
        block = (peer % 2) * 16 + (peer // 2 % 4) * 4 + peer // 8
        return remote(
            tap.at[block], tap_out.at[me], tap_send.at[step], tap_recv.at[step],
            {"facet": peer // 2, "vis": peer % 2},
        )

    def tap_arrival(step):
        source = (me - step + 32) % 32
        return remote(
            tap.at[0], tap_out.at[source], tap_send.at[step], tap_recv.at[step],
            {"facet": source // 2, "vis": source % 2},
        )

    def after_core(dz):
        core_copy(dz).wait()
        part[dz, c] = part[dz, c] + got_core[dz]
        for dy in (2, 1, 3):
            y_copy(dz, dy).start()

    def after_y(dz):
        for dy in (1, 3, 2):
            y_copy(dz, dy).wait()
        tot[dz] = (part[dz, c, y] + got_y[dz, 0]) + (got_y[dz, 1] + got_y[dz, 2])
        if dz == 2:
            far_copy(0).start()
            far_copy(1).start()

    def after_far(side):
        far_copy(side).wait()
        half, dz = (last, 3) if side else (first, 1)
        tot[dz, half] = tot[dz, half] + got_far[side]
        z_copy(side).start()

    rows = core * 256 + iota((8, 256), 1)
    r_re, r_im = turned(sub * 4099 * rows, 65536)
    r_re, r_im = r_re[0:1], r_im[0:1]
    freq = iota((16, 512), 1)
    other = iota((16, 512), 0)
    turn = facet * ((freq + 5 * other + 6 * sub) & 15) * 16 + freq * core
    w_re, w_im = turned(turn, 256)
    w_re, w_im = (w_re * SCALE)[None], (w_im * SCALE)[None]

    def finish(dz):
        a_re = (acc[:256, :128] - acc[256:, 128:]).T
        a_im = (acc[:256, 128:] + acc[256:, :128]).T
        both = jnp.concatenate([a_re * r_re - a_im * r_im, a_re * r_im + a_im * r_re], 1)
        prod = dot3(both, lh_ref[...], ll_ref[...])
        o_re = prod[:, :512].reshape(8, 16, 512)
        o_im = prod[:, 512:].reshape(8, 16, 512)
        part[dz, :, :, 0:16, :] = (o_re * w_re - o_im * w_im).reshape(2, 4, 16, 512)
        part[dz, :, :, 16:32, :] = (o_re * w_im + o_im * w_re).reshape(2, 4, 16, 512)

    def apart(step, value):
        def body(index, carry):
            step(value)
            return carry

        lax.fori_loop(0, 1 + facet // 16, body, 0)

    def multiply(dz, where):
        high, low = xh[:, where], xl[:, where]
        t_high, t_low = th[dz, where, :], tl[dz, where, :]
        return dot(high, t_high) + dot(low, t_high) + dot(high, t_low)

    def prepare(index):
        where = slice(index * WIDTH, index * WIDTH + WIDTH)
        cols = index * WIDTH + iota((8, WIDTH), 1)
        c_re, c_im = turned(sub * 1031 * cols, 65536)
        c_re, c_im = c_re[0:1], c_im[0:1]
        s_re, s_im = raw[:, where], raw[:, slice(2048 + where.start, 2048 + where.stop)]
        for half, moved in enumerate((s_re * c_re - s_im * c_im, s_re * c_im + s_im * c_re)):
            high, low = split(moved)
            xh[half * 256 : half * 256 + 256, where] = high
            xl[half * 256 : half * 256 + 256, where] = low

    cut = cut_taper(window[...])
    tap[:, 0, :] = cut[:, :128]
    tap[:, 1, :] = cut[:, 128:]
    picks[...] = jnp.zeros_like(picks)
    for other_z in range(4):
        for other_x in range(4):
            value = pick_ref[other_x * 4 + other_z].astype(F32)
            picks[other_z, other_x : other_x + 1, :] = jnp.full((1, 128), value, F32)

    for index in range(PIECES):
        for copy in piece_copies(index):
            copy.wait()
        if index:
            for copy in t_copies(order[index]):
                copy.start()
        apart(prepare, index)
        def piece(index):
            more = multiply(order[0], slice(index * WIDTH, (index + 1) * WIDTH))
            acc[...] = more if index == 0 else acc[...] + more
        apart(piece, index)
    for copy in late[:2]:
        copy.wait()
    for copy in late[2:]:
        copy.start()
    apart(finish, 2)
    pl.semaphore_wait(barrier, 37)
    core_copy(2).start()

    def tap_start(step, carry):
        tap_copy(step).start()
        return carry


    def chunk(dz, between):
        for copy in t_copies(dz):
            copy.wait()
        acc[...] = multiply(dz, slice(0, 1024))
        between()
        acc[...] += multiply(dz, slice(1024, 2048))
        apart(finish, dz)
        core_copy(dz).start()

    chunk(1, lambda: after_core(2))

    def between_three():
        after_core(1)
        after_y(2)

    chunk(3, between_three)

    def between_four():
        after_core(3)
        after_y(1)

    chunk(0, between_four)
    lax.fori_loop(1, 32, tap_start, 0)
    tap_out[me] = tap[c * 16 + y * 4 + z]
    after_core(0)
    after_far(0)
    after_y(3)
    after_far(1)

    def tap_wait(step, carry):
        tap_copy(step).wait_send()
        tap_arrival(step).wait_recv()
        return carry

    lax.fori_loop(1, 32, tap_wait, 0)
    taper = placed_taper(tap_out[...])
    after_y(0)
    z_copy(0).wait()
    z_copy(1).wait()
    sums = tot[0] + (got_z[0] + got_z[1])

    for copy in late[2:]:
        copy.wait()

    tapered = sums * jnp.concatenate([taper, taper], 0)
    prod = dot3(tapered, ph[...], pw[...])
    for block in range(8):
        where = slice(block * 128, block * 128 + 128)
        ubuf[block // 2, block % 2] = swapped(prod[:16, where], prod[16:, where])

    def uz_copy(dz):
        to = (z + dz) % 4
        return remote(
            ubuf.at[to], zbuf.at[z], uz_send.at[dz - 1], uz_recv.at[dz - 1], {"facet": to * 4 + y}
        )

    def uz_arrival(dz):
        source = (z - dz + 4) % 4
        return remote(
            ubuf.at[source], zbuf.at[source], uz_send.at[dz - 1], uz_recv.at[dz - 1],
            {"facet": source * 4 + y},
        )

    def uy_copy(index, dz):
        dy, dc = near[index]
        to = (y + dy) % 4
        source = (z - dz + 4) % 4
        return remote(
            zbuf.at[source, to // 2], ybuf.at[c, y, source], uy_send.at[index, dz],
            uy_recv.at[index, dz], {"facet": z * 4 + to, "vis": (c + dc) % 2},
        )

    def uy_arrival(index, dz):
        dy, dc = near[index]
        origin = (y - dy + 4) % 4
        source = (z - dz + 4) % 4
        return remote(
            zbuf.at[source, 0], ybuf.at[(c + dc) % 2, origin, source], uy_send.at[index, dz],
            uy_recv.at[index, dz], {"facet": z * 4 + origin, "vis": (c + dc) % 2},
        )

    for dz in (2, 1, 3):
        uz_copy(dz).start()
    zbuf[z] = ubuf[z]
    for dz in (0, 1, 3, 2):
        if dz:
            uz_arrival(dz).wait_recv()
        for index in (4, 3, 2, 1, 6, 5, 0):
            uy_copy(index, dz).start()
    ybuf[c, y] = zbuf[:, y // 2]
    for dz in (1, 2, 3):
        uz_copy(dz).wait_send()
    for dz in (0, 1, 3, 2):
        for index in range(7):
            uy_copy(index, dz).wait_send()
            uy_arrival(index, dz).wait_recv()
    cols = ybuf[...].reshape(512, 128).T
    where = pl.ds(pl.multiple_of(((y % 2) * 2 + c) * 256, 256), 256)
    prod = dot3(cols, ph[:, where], pw[:, where])
    for j in range(2):
        where = slice(j * 128, j * 128 + 128)
        own[j] = swapped(prod[:64, where], prod[64:, where])

    def w_copies(dz):
        to = (w + dz) % 4
        device = {"sub": x * 4 + to}
        return (
            remote(own, zpatch.at[dz - 1], w_send.at[dz - 1], w_recv.at[dz - 1], device),
            remote(picks.at[to], zpick.at[dz - 1], p_send.at[dz - 1], p_recv.at[dz - 1], device),
        )

    def x_copy(dx, dz):
        source = (w - dz + 4) % 4
        return remote(
            staged.at[dx - 1, dz], out.at[x * 4 + source], x_send.at[dx - 1, dz],
            x_recv.at[dx - 1, dz], {"sub": (x + dx) % 4 * 4 + w},
        )

    def x_arrival(dx, dz):
        origin = (x - dx + 4) % 4
        source = (w - dz + 4) % 4
        return remote(
            staged.at[dx - 1, dz], out.at[origin * 4 + source], x_send.at[dx - 1, dz],
            x_recv.at[dx - 1, dz], {"sub": origin * 4 + w},
        )

    cells = iota((64, 1024), 0)

    def mark(unused):
        for base in range(8):
            hot[base] = ones_where(cells == offsets[base, 0:1, :])

    for dz in (2, 1, 3):
        for copy in w_copies(dz):
            copy.start()
    for dz in (0, 1, 3, 2):
        source = (w - dz + 4) % 4
        if dz:
            for copy in w_copies(dz):
                copy.wait_recv()
            first, second, table = zpatch[dz - 1, 0], zpatch[dz - 1, 1], zpick.at[dz - 1]
        else:
            first, second, table = own[0], own[1], picks.at[w]
        for dx in (2, 1, 3, 0):
            chosen = table[pl.ds((x + dx) % 4, 1), :]
            value = jnp.where(jnp.broadcast_to(chosen, first.shape) > 0.5, second, first)
            if dx:
                staged[dx - 1, dz] = value
                x_copy(dx, dz).start()
            else:
                out[x * 4 + source] = value
        if dz == 0:
            apart(mark, 0)
    for dz in (1, 2, 3):
        for copy in w_copies(dz):
            copy.wait_send()
    for dz in (0, 1, 3, 2):
        for dx in (1, 3, 2):
            x_copy(dx, dz).wait_send()
            x_arrival(dx, dz).wait_recv()
    degrid(owners, out, tiles, offsets, hot, eh, el, fh, fl, vis)


def predicted(strip, window, pick_row, owners, tiles, offsets):
    dma = pltpu.SemaphoreType.DMA
    column = [jnp.asarray(x) for x in column_table()]
    rest = [jnp.asarray(x) for x in row_table() + grid_table()]
    cells = [jnp.asarray(x) for x in cell_tables()]
    far = pl.BlockSpec(memory_space=pl.ANY)
    small = pl.BlockSpec(memory_space=pltpu.SMEM)
    return pl.pallas_call(
        patch_kernel,
        out_shape=jax.ShapeDtypeStruct((8, 2, 1024), F32),
        in_specs=[far] * 3 + [VM, small, small] + [far] * 10,
        out_specs=VM,
        scratch_shapes=[
            pltpu.VMEM((512, 1024), BF16),
            pltpu.VMEM((512, 1024), BF16),
            pltpu.VMEM((512, 1024), BF16),
            pltpu.VMEM((512, 1024), BF16),
            pltpu.VMEM((8, 64, 128), F32),
            pltpu.VMEM((8, 2, 1024), jnp.int32),
            pltpu.VMEM((128, 128), BF16),
            pltpu.VMEM((128, 128), BF16),
            pltpu.VMEM((64, 128), BF16),
            pltpu.VMEM((64, 128), BF16),
            pltpu.VMEM((16, 64, 128), F32),
            pltpu.VMEM((8, 64, 1024), BF16),
            pltpu.VMEM((32, 2, 128), F32),
            pltpu.VMEM((512, 256), F32),
            pltpu.VMEM((256, 4096), F32),
            pltpu.VMEM((512, 2048), BF16),
            pltpu.VMEM((512, 2048), BF16),
            pltpu.VMEM((4, 2048, 256), BF16),
            pltpu.VMEM((4, 2048, 256), BF16),
            pltpu.VMEM((4, 2, 4, 32, 512), F32),
            pltpu.VMEM((4, 4, 32, 512), F32),
            pltpu.VMEM((4, 3, 32, 512), F32),
            pltpu.VMEM((4, 32, 512), F32),
            pltpu.VMEM((2, 16, 512), F32),
            pltpu.VMEM((2, 32, 512), F32),
            pltpu.VMEM((32, 2, 128), F32),
            pltpu.VMEM((4, 2, 16, 128), F32),
            pltpu.VMEM((4, 2, 16, 128), F32),
            pltpu.VMEM((2, 4, 4, 16, 128), F32),
            pltpu.VMEM((2, 64, 128), F32),
            pltpu.VMEM((4, 8, 128), F32),
            pltpu.VMEM((3, 2, 64, 128), F32),
            pltpu.VMEM((3, 8, 128), F32),
            pltpu.VMEM((3, 4, 64, 128), F32),
            dma((10,)), dma((PIECES, 4)), dma((4, 2)),
            dma((4,)), dma((4,)), dma((4, 3)), dma((4, 3)), dma((2,)), dma((2,)), dma((2,)), dma((2,)),
            dma((32,)), dma((32,)),
            dma((3,)), dma((3,)), dma((7, 4)), dma((7, 4)),
            dma((3,)), dma((3,)), dma((3,)), dma((3,)), dma((3, 4)), dma((3, 4)),
        ],
        compiler_params=pltpu.CompilerParams(
            collective_id=0, has_side_effects=True, vmem_limit_bytes=58 << 20
        ),
    )(strip, *column, window, pick_row, owners, *rest, tiles, offsets, *cells)


def local(facet_strips, taper, send_pick, bl_owner, phase_tiles, cell_offsets):
    result = predicted(
        facet_strips[0], taper[0], send_pick[0, 0, 0], bl_owner[0, 0, 0],
        phase_tiles[0, 0, 0], cell_offsets[0, 0, 0],
    )
    return result[None, None, None]


def solution(mesh):
    placed = (
        P("facet", "vis", None),
        P("sub", ("facet", "vis"), None),
        P("facet", "sub", "vis", None),
        P("facet", "sub", "vis", None),
        P("facet", "sub", "vis", None, None, None),
        P("facet", "sub", "vis", None, None, None),
    )
    return jax.shard_map(
        local,
        mesh=mesh,
        in_specs=placed,
        out_specs=P("facet", "sub", "vis", None, None, None),
        check_vma=False,
    )
```
